128 devices in a mesh: dp: 8 (over x, core), mp: 16 (over z, y).
Axes of the slice: x: 4, y: 4, z: 4, core: 2. Of those that a mesh axis runs over, the one named last changes fastest.
Arguments:
- queries: bfloat16 [1024, 4096], P('dp', 'mp'), may hold values from -48 to 48
- passages: bfloat16 [1024, 4096], P('dp', 'mp'), may hold values from -12 to 12
- pool_rows: bfloat16 [65536, 4096], P(('dp', 'mp')), may hold values from -6 to 6
- negatives: int32 [1024, 31], P(('dp', 'mp')), may hold values from 0 to 65535, as said below
Outputs:
- mean_loss: float32 [], replicated
- grad_queries: bfloat16 [1024, 4096], P('dp', 'mp')
- grad_passages: bfloat16 [1024, 4096], P('dp', 'mp')
- grad_pool: bfloat16 [65536, 4096], P(('dp', 'mp'))
The draws below stay inside these ranges and needn't reach their ends.
Inputs may be any that keep to these rules, and one draw needn't show every extreme that they name: `negatives`: row r of the pool lies on device r // 512 in dp+mp order. Among the 248 pairs of one device's queries, at most 4 name rows of one device; in every draw some device is named by exactly 4 pairs of every device's queries. A query may name one row more than once.
All inputs are finite; a program needn't handle non-finite values.
Results may differ from the reference program's by a relative error of at most 0.017.
Values may be sent and summed in bfloat16 or wider, within the bound.
A program may use at most 128 MiB of HBM per device.

```python
import math
import jax
import jax.numpy as jnp
from jax import lax

D = 4096
NEGS = 31
Q_DEV = 128
POOL_DEV = 512
BATCH = 1024
POOL = 65536
N_DP = 8
N_MP = 16


def passage_matrix(key, twin):
    base_rows = jnp.clip(jax.random.normal(jax.random.fold_in(key, 7001), (BATCH, D), jnp.float32), -4.0, 4.0)
    scaled = base_rows
    twin_pick = (jnp.arange(BATCH) % 256 == 1).astype(jnp.float32)[:, None] * twin
    return scaled * (1.0 - twin_pick)


def draw_passages(key, part):
    shared = key
    matrix = passage_matrix(shared, 0.0)
    return matrix.astype(jnp.bfloat16)


def draw_queries(key, part):
    key = jax.random.fold_in(key, 23)
    own_rows = jnp.clip(jax.random.normal(key, (BATCH, D), jnp.float32), -4.0, 4.0)
    result = own_rows
    return result.astype(jnp.bfloat16)


def draw_negatives(key, part):
    key = jax.random.fold_in(key, 5)
    devices = N_DP * N_MP
    qrows = Q_DEV // N_MP
    pairs = qrows * NEGS
    slots = max(2, 12 * pairs // (5 * devices))
    common_key = jax.random.fold_in(key, 99)
    hot_owner = jax.random.randint(common_key, (), 0, devices)

    def one_device(dev_key):
        first_key, second_key, third_key = jax.random.split(dev_key, 3)
        owner_perm = jax.random.permutation(first_key, devices)
        head_owner = owner_perm[0]
        owner_perm = jnp.where(owner_perm == hot_owner, head_owner, owner_perm)
        owner_perm = owner_perm.at[0].set(hot_owner)
        positions = jnp.arange(pairs)
        owner_rank = jnp.where(positions < 4 * slots, positions // slots, 4 + (positions - 4 * slots) % (devices - 4))
        owners = owner_perm[owner_rank]
        owners = owners[jax.random.permutation(second_key, pairs)]
        row_within = jax.random.randint(third_key, (pairs,), 0, POOL_DEV)
        return (owners * POOL_DEV + row_within).astype(jnp.int32).reshape(qrows, NEGS)
    dev_keys = jax.random.split(key, devices)
    return jax.vmap(one_device)(dev_keys).reshape(devices * qrows, NEGS)


def steps_of(own_key, extent, pieces, smallest, high):
    def one(position, shards_of):
        draws = jax.random.uniform(jax.random.fold_in(jax.random.fold_in(own_key, 6), position), (shards_of,), jnp.float32, smallest / len(pieces), high / len(pieces))
        return jnp.repeat(jnp.exp(draws), extent[position] // shards_of).reshape((-1,) + (1,) * (len(extent) - position - 1))

    level = one(*pieces[0])
    for cut in pieces[1:]:
        level = level * one(*cut)
    return level


def scatter_about(rng, extent, scale, most, pieces=(), kind=jnp.bfloat16):
    values = jax.random.normal(rng, extent, jnp.float32) * scale
    if len(pieces) > 0:
        values = steps_of(rng, extent, pieces, -0.22, 0.18) * values
    return jnp.clip(values, min=-most, max=most).astype(kind)


def setup_inputs(seed: int = 0) -> dict:
    arg_keys = jax.random.split(jax.random.key(seed), 5)
    queries = draw_queries(jax.random.fold_in(arg_keys[4], 71), 0)
    passages = draw_passages(jax.random.fold_in(arg_keys[4], 71), 0)
    pool_rows = scatter_about(arg_keys[2], (POOL, D), 1.0, 6.0, ((0, 128),))
    negatives = draw_negatives(jax.random.fold_in(arg_keys[4], 71), 0)
    return {"queries": queries, "passages": passages, "pool_rows": pool_rows, "negatives": negatives}


def reference(queries, passages, pool_rows, negatives):
    inverse_square_root = 1.0 / math.sqrt(D)
    inbatch = jnp.dot(queries, passages.T, preferred_element_type=jnp.float32) * inverse_square_root
    query_blocks = queries.reshape(N_DP, Q_DEV, D)
    index_blocks = negatives.reshape(N_DP, Q_DEV, NEGS)

    def hard_scores(pair):
        query_block_local, index_block = pair
        received_rows = jnp.take(pool_rows, index_block, axis=0)
        return jnp.einsum('oa,ofa->of', query_block_local.astype(jnp.float32), received_rows.astype(jnp.float32)) * inverse_square_root
    hard = lax.map(hard_scores, (query_blocks, index_blocks)).reshape(BATCH, NEGS)
    logits = jnp.concatenate([inbatch, hard], axis=1)
    highest = lax.optimization_barrier(jnp.max(logits, axis=1, keepdims=True))
    log_total = highest + jnp.log(lax.optimization_barrier(jnp.sum(jnp.exp(logits - highest), axis=1, keepdims=True)))
    positive = jnp.diagonal(inbatch)
    mean_loss = jnp.sum(log_total[:, 0] - positive) / BATCH
    probs = jnp.exp(logits - log_total)
    identity = jnp.eye(BATCH, dtype=jnp.float32)
    grad_inbatch = ((probs[:, :BATCH] - identity) / BATCH).astype(jnp.bfloat16)
    gradient_hard_negatives = (probs[:, BATCH:] / BATCH).astype(jnp.bfloat16)
    grad_blocks = gradient_hard_negatives.reshape(N_DP, Q_DEV, NEGS)

    def hard_back(pair):
        gradient_block_part, index_block = pair
        received_rows = jnp.take(pool_rows, index_block, axis=0)
        return jnp.einsum('ei,eic->ec', gradient_block_part.astype(jnp.float32), received_rows.astype(jnp.float32))
    query_hard_scores = lax.map(hard_back, (grad_blocks, index_blocks)).reshape(BATCH, D)
    inbatch_part = jnp.dot(grad_inbatch, passages, preferred_element_type=jnp.float32)
    grad_queries = ((inbatch_part + query_hard_scores) * inverse_square_root).astype(jnp.bfloat16)
    grad_passages = (jnp.dot(grad_inbatch.T, queries, preferred_element_type=jnp.float32) * inverse_square_root).astype(jnp.bfloat16)

    def pool_add(accum, triple):
        query_block_local, index_block, gradient_block_part = triple
        terms = (gradient_block_part.astype(jnp.float32)[:, :, None] * query_block_local.astype(jnp.float32)[:, None, :] * inverse_square_root).astype(jnp.bfloat16)
        accum = accum.at[index_block.reshape(-1)].add(terms.reshape(-1, D).astype(jnp.float32))
        return (accum, None)
    accum, unused = lax.scan(pool_add, jnp.zeros((POOL, D), jnp.float32), (query_blocks, index_blocks, grad_blocks))
    grad_pool = accum.astype(jnp.bfloat16)
    return (mean_loss, grad_queries, grad_passages, grad_pool)
```

```python
import jax
import jax.numpy as jnp
from jax import lax
from jax.experimental import pallas as pl
from jax.experimental.pallas import tpu as pltpu
from jax.sharding import PartitionSpec as P

MESH = pl.DeviceIdType.MESH
F32 = jnp.float32
BF16 = jnp.bfloat16

D = 4096
NEGS = 31
BATCH = 1024
ROWS = 512
PLANE = 512
SCALE = 1.0 / 64.0
ORDERS = ("xyz", "yzx", "zxy")
PART_OFF = (0, 48, 96)
AG_ROWS = 48
RS_ROWS = (48, 48, 32)
LOW = -1e30


def kernel(
    q_ref, p_ref, pool_ref, neg_ref,
    loss_ref, gq_ref, gp_ref, gpool_ref,
    ag0, ag1, ag2, pool, queries, pas_rx, pas, scores, pscores, names, et, pet, wd, wx, fcol,
    stats, loss_own, loss_sib, gp_tx, gp_rx, out,
    d0, d1, d2,
    h0a, h0b, h0c, h0d, f0a, f0b, f0c, f0d, i0a, i0b, g0a, g0b,
    h1a, h1b, h1c, h1d, f1a, f1b, f1c, f1d, i1a, i1b, g1a, g1b,
    h2a, h2b, h2c, h2d, f2a, f2b, f2c, f2d, i2a, i2b, g2a, g2b,
    local_sem, pool_send, pool_recv, ag_send, ag_recv, pas_send, pas_recv, q_send, q_recv,
    st_send, st_recv, w_send, w_recv, rs_send, rs_recv, gp_send, gp_recv, loss_send, loss_recv, out_sem,
):
    dp = lax.axis_index("dp")
    mp = lax.axis_index("mp")
    core = lax.rem(dp, 2)
    at = {"x": dp // 2, "y": lax.rem(mp, 4), "z": mp // 4}
    zy = mp
    sib = (at["x"] * 2 + 1 - core, mp)

    def peer(axis, delta):
        there = dict(at)
        there[axis] = lax.rem(at[axis] + delta, 4)
        return (there["x"] * 2 + core, there["z"] * 4 + there["y"])

    def send(src, dst, send_sem, recv_sem, device):
        copy = pltpu.make_async_remote_copy(
            src_ref=src, dst_ref=dst, send_sem=send_sem, recv_sem=recv_sem,
            device_id=device, device_id_type=MESH,
        )
        copy.start()
        return copy

    def arrived(ref, sem):
        pltpu.make_async_copy(ref, ref, sem).wait()

    barrier = pltpu.get_barrier_semaphore()
    for axis in "xyz":
        for delta in (1, 3):
            pl.semaphore_signal(barrier, inc=1, device_id=peer(axis, delta), device_id_type=MESH)
    pl.semaphore_signal(barrier, inc=1, device_id=sib, device_id_type=MESH)
    pl.semaphore_wait(barrier, 7)

    pending = []

    ags = (ag0, ag1, ag2)

    def slot(part):
        a, b, c = ORDERS[part]
        return at[c], at[b], at[a]

    c, b, a = slot(0)
    ag0[c, b, a] = q_ref[0:48, :]
    c, b, a = slot(1)
    ag1[c, b, a] = q_ref[48:96, :]
    c, b, a = slot(2)
    ag2[c, b, a, 0:32] = q_ref[96:128, :]
    ids = neg_ref[...]
    high = (ids >> 8).astype(F32)
    low = (ids & 255).astype(F32)
    ag2[c, b, a, 32:48] = jnp.concatenate([high, low], axis=0).astype(BF16)

    def ag_blocks(part, phase):
        buf = ags[part]
        c, b, a = slot(part)
        if phase == 0:
            return lambda g: buf.at[c, b, g], lambda g, h: buf.at[c, b, g, :, 128 * h : 128 * h + 128]
        if phase == 1:
            return lambda g: buf.at[c, g], lambda g, h: buf.at[c, g, 2 * h : 2 * h + 2]
        return lambda g: buf.at[g], lambda g, h: buf.at[g, 2 * h : 2 * h + 2]

    def ag_phase(phase):
        views = []
        for part in range(3):
            axis = ORDERS[part][phase]
            block, half = ag_blocks(part, phase)
            g = at[axis]
            k = (part * 3 + phase) * 4
            right, left = peer(axis, 1), peer(axis, 3)
            pending.append(send(block(g), block(g), ag_send.at[k], ag_recv.at[k], right))
            pending.append(send(block(g), block(g), ag_send.at[k + 1], ag_recv.at[k + 1], left))
            views.append((block, half, g, k, right, left))
        for block, half, g, k, right, left in views:
            before, after = lax.rem(g + 3, 4), lax.rem(g + 1, 4)
            arrived(block(before), ag_recv.at[k])
            pending.append(send(half(before, 0), half(before, 0), ag_send.at[k + 2], ag_recv.at[k + 2], right))
            arrived(block(after), ag_recv.at[k + 1])
            pending.append(send(half(after, 1), half(after, 1), ag_send.at[k + 3], ag_recv.at[k + 3], left))
        for block, half, g, k, right, left in views:
            far = lax.rem(g + 2, 4)
            arrived(half(far, 0), ag_recv.at[k + 2])
            arrived(half(far, 1), ag_recv.at[k + 3])

    ag_phase(0)
    own_pool = pltpu.make_async_copy(pool_ref, pool.at[0:ROWS], local_sem)
    own_pool.start()
    pool_copy = send(pool_ref, pool.at[ROWS : 2 * ROWS], pool_send, pool_recv, sib)
    ag_phase(1)

    for t in range(8):
        for other in range(2):
            chip = core * 8 + t
            target = (at["x"] * 2 + other, chip)
            me = jnp.logical_and(chip == zy, core == other)
            src = p_ref.at[16 * t : 16 * t + 16]
            dst = pas_rx.at[zy]
            k = t * 2 + other

            @pl.when(me)
            def _():
                pltpu.make_async_copy(src, dst, pas_recv.at[zy]).start()

            @pl.when(jnp.logical_not(me))
            def _():
                send(src, dst, pas_send.at[k], pas_recv.at[zy], target)

    ag_phase(2)

    def assemble(i, _):
        z, y = i // 4, lax.rem(i, 4)
        cols = pl.ds(pl.multiple_of(i * 256, 256), 256)
        for x in range(4):
            where = {"x": x, "y": y, "z": z}
            for part in range(3):
                aa, bb, cc = ORDERS[part]
                rows = RS_ROWS[part]
                start = x * 128 + PART_OFF[part]
                queries[start : start + rows, cols] = ags[part][where[cc], where[bb], where[aa], 0:rows]
        return 0

    lax.fori_loop(0, 16, assemble, 0)
    q_copy = send(queries.at[0:PLANE], queries.at[PLANE : 2 * PLANE], q_send, q_recv, sib)

    for i in range(16):
        arrived(pas_rx.at[i], pas_recv.at[i])
        pas[:, 256 * i : 256 * i + 256] = pas_rx[i]

    mine = dp * 16 + mp
    theirs = (at["x"] * 2 + 1 - core) * 16 + mp
    sub = lax.broadcasted_iota(jnp.int32, (128, 128), 0)
    for x in range(4):
        pieces = []
        for i in range(16):
            where = {"x": x, "y": i % 4, "z": i // 4}
            aa, bb, cc = ORDERS[2]
            tile = ag2[where[cc], where[bb], where[aa], 32:48, 0:128].astype(F32)
            pieces.append(tile[0:8] * 256.0 + tile[8:16])
        named = jnp.concatenate(pieces, axis=0).T[0:32].astype(jnp.int32)
        owner = named >> 9
        field = ((named >> 7) & 3) * 4
        bit = jnp.where(
            owner == mine, jnp.left_shift(1, field),
            jnp.where(owner == theirs, jnp.left_shift(1, field + 16), 0),
        )
        hi = named & 127
        packed = jnp.zeros((128, 128), jnp.int32)
        for k in range(NEGS):
            packed = packed + jnp.where(sub == hi[k : k + 1], bit[k : k + 1], 0)
        names[:, 128 * x : 128 * x + 128] = packed

    own_pool.wait()
    pool_copy.wait_recv()
    contract = (((1,), (1,)), ((), ()))
    scores[...] = jnp.zeros_like(scores)

    def score(i, _):
        cols = pl.ds(pl.multiple_of(i * 1024, 1024), 1024)
        scores[...] += lax.dot_general(pool[:, cols], queries[0:PLANE, cols], contract, preferred_element_type=F32)
        return 0

    lax.fori_loop(0, 4, score, 0)
    ps = lax.dot_general(pas[...], queries[0:PLANE, :], contract, preferred_element_type=F32) * SCALE

    lane = lax.broadcasted_iota(jnp.int32, (16, PLANE), 1)
    psub = lax.broadcasted_iota(jnp.int32, (16, PLANE), 0)
    in_plane = core == zy // 8
    first = jnp.where(in_plane, at["x"] * 128 + lax.rem(zy, 8) * 16, -1024)
    same = lane == first + psub
    pos = jnp.sum(jnp.where(same, ps, 0.0), axis=0, keepdims=True)

    def count_of(f):
        return (names[...] >> (4 * f)) & 15

    top = jnp.max(ps, axis=0, keepdims=True)
    for f in range(8):
        s = jnp.where(count_of(f) > 0, scores[128 * f : 128 * f + 128] * SCALE, LOW)
        scores[128 * f : 128 * f + 128] = s
        top = jnp.maximum(top, jnp.max(s, axis=0, keepdims=True))
    pe = jnp.exp(ps - top)
    pscores[...] = pe
    total = jnp.sum(pe, axis=0, keepdims=True)
    for f in range(8):
        e = jnp.exp(scores[128 * f : 128 * f + 128] - top) * count_of(f).astype(F32)
        scores[128 * f : 128 * f + 128] = e
        total = total + jnp.sum(e, axis=0, keepdims=True)
        et[:, 128 * f : 128 * f + 128] = e.T.astype(BF16)
    pet[...] = pe.T.astype(BF16)

    filler = jnp.zeros((5, PLANE), F32)
    whole = jnp.concatenate([top, total, pos, filler], axis=0)
    for n, axis in enumerate("xyz"):
        g = at[axis]
        stats[n, g] = whole
        for delta in (1, 2, 3):
            k = n * 4 + delta
            pending.append(send(
                stats.at[n, g], stats.at[n, g], st_send.at[k],
                st_recv.at[k], peer(axis, delta),
            ))
        for delta in (1, 2, 3):
            arrived(stats.at[n, lax.rem(g + 4 - delta, 4)], st_recv.at[n * 4 + delta])
        parts = [stats[n, i] for i in range(4)]
        best = parts[0][0:1]
        for i in range(1, 4):
            best = jnp.maximum(best, parts[i][0:1])
        summed = jnp.zeros_like(best)
        positive = jnp.zeros_like(best)
        for i in range(4):
            summed = summed + parts[i][1:2] * jnp.exp(parts[i][0:1] - best)
            positive = positive + parts[i][2:3]
        whole = jnp.concatenate([best, summed, positive, filler], axis=0)
    log_total = best + jnp.log(summed)
    loss_own[...] = jnp.broadcast_to(jnp.sum(log_total - positive, axis=1, keepdims=True), (8, 128))
    loss_copy = send(loss_own, loss_sib, loss_send, loss_recv, sib)
    factor = jnp.exp(top - log_total) / BATCH

    wp = (pscores[...] * factor - jnp.where(same, 1.0 / BATCH, 0.0)).astype(BF16)
    wx[0:ROWS] = (scores[ROWS : 2 * ROWS] * factor).astype(BF16)
    wx[ROWS : ROWS + 16] = wp
    w_copy = send(wx, wd.at[:, PLANE : 2 * PLANE], w_send, w_recv, sib)
    wd[0:ROWS, 0:PLANE] = (scores[0:ROWS] * factor).astype(BF16)
    wd[ROWS : ROWS + 16, 0:PLANE] = wp

    wide = jnp.broadcast_to(factor * SCALE, (128, PLANE))
    for x in range(4):
        fcol[128 * x : 128 * x + 128] = wide[:, 128 * x : 128 * x + 128].T

    ds = (d0, d1, d2)
    own_row = pl.multiple_of(jnp.where(in_plane, first, 0), 16)

    def back(i, _):
        z, y = i // 4, lax.rem(i, 4)
        cols = pl.ds(pl.multiple_of(i * 256, 256), 256)
        right = pool[:, cols]
        pright = pas[:, cols]
        own_piece = jnp.where(in_plane, pright.astype(F32) * (SCALE / BATCH), 0.0)
        for x in range(4):
            rows = slice(128 * x, 128 * x + 128)
            acc = jnp.dot(et[rows], right, preferred_element_type=F32)
            acc = acc + jnp.dot(pet[rows], pright, preferred_element_type=F32)
            f = fcol[rows]
            acc = acc * jnp.concatenate([f, f], axis=1)
            placed = jnp.concatenate([own_piece] * 8, axis=0)
            r = lax.broadcasted_iota(jnp.int32, (128, 256), 0) + 128 * x
            hit = jnp.logical_and(r >= own_row, r < own_row + 16)
            acc = acc - jnp.where(hit, placed, 0.0)
            acc = acc.astype(BF16)
            where = {"x": x, "y": y, "z": z}
            for part in range(3):
                aa, bb, cc = ORDERS[part]
                o = PART_OFF[part]
                ds[part][where[cc], where[bb], where[aa]] = acc[o : o + RS_ROWS[part]]
        return 0

    lax.fori_loop(0, 16, back, 0)

    bufs = (
        (((h0a, h0b, f0a, f0b), (h0c, h0d, f0c, f0d), (i0a, i0b, g0a, g0b))),
        (((h1a, h1b, f1a, f1b), (h1c, h1d, f1c, f1d), (i1a, i1b, g1a, g1b))),
        (((h2a, h2b, f2a, f2b), (h2c, h2d, f2c, f2d), (i2a, i2b, g2a, g2b))),
    )

    def add_into(dst, srcs, lead):
        if len(lead) == 0:
            total = dst[...].astype(F32)
            for src in srcs:
                total = total + src[...].astype(F32)
            dst[...] = total.astype(BF16)
            return
        count = 1
        for n in lead:
            count *= n

        def body(i, _):
            index = (i,) if len(lead) == 1 else (i // lead[1], lax.rem(i, lead[1]))
            total = dst[index].astype(F32)
            for src in srcs:
                total = total + src[index].astype(F32)
            dst[index] = total.astype(BF16)
            return 0

        lax.fori_loop(0, count, body, 0)

    def rs_views(part, phase):
        buf = ds[part]
        c, b, a = slot(part)
        if phase == 0:
            return lambda g: buf.at[g], lambda g, h: buf.at[g, 2 * h : 2 * h + 2], (2, 4), (4, 4)
        if phase == 1:
            return lambda g: buf.at[c, g], lambda g, h: buf.at[c, g, 2 * h : 2 * h + 2], (2,), (4,)
        return lambda g: buf.at[c, b, g], lambda g, h: buf.at[c, b, g, :, 128 * h : 128 * h + 128], (), ()

    def rs_phase(phase):
        views = []
        for part in range(3):
            axis = ORDERS[part][2 - phase]
            block, half, half_lead, lead = rs_views(part, phase)
            hl, hr, fl, fr = bufs[part][phase]
            g = at[axis]
            k = (part * 3 + phase) * 4
            right, left = peer(axis, 1), peer(axis, 3)
            far = lax.rem(g + 2, 4)
            pending.append(send(half(far, 0), hl, rs_send.at[k], rs_recv.at[k], right))
            pending.append(send(half(far, 1), hr, rs_send.at[k + 1], rs_recv.at[k + 1], left))
            views.append((block, half, half_lead, lead, g, k, right, left, hl, hr, fl, fr))
        for block, half, half_lead, lead, g, k, right, left, hl, hr, fl, fr in views:
            before, after = lax.rem(g + 3, 4), lax.rem(g + 1, 4)
            arrived(hl, rs_recv.at[k])
            add_into(half(after, 0), (hl,), half_lead)
            pending.append(send(block(after), fl, rs_send.at[k + 2], rs_recv.at[k + 2], right))
            arrived(hr, rs_recv.at[k + 1])
            add_into(half(before, 1), (hr,), half_lead)
            pending.append(send(block(before), fr, rs_send.at[k + 3], rs_recv.at[k + 3], left))
        return views

    def rs_finish(views):
        for block, half, half_lead, lead, g, k, right, left, hl, hr, fl, fr in views:
            arrived(fl, rs_recv.at[k + 2])
            arrived(fr, rs_recv.at[k + 3])
            add_into(block(g), (fl, fr), lead)

    views = rs_phase(0)

    q_copy.wait_recv()
    w_copy.wait_recv()

    def pool_grad(i, _):
        cols = pl.ds(pl.multiple_of(i * 512, 512), 512)
        acc = jnp.dot(wd[...], queries[:, cols], preferred_element_type=F32) * SCALE
        out[:, cols] = acc[0:ROWS].astype(BF16)
        gp_tx[:, cols] = acc[ROWS : ROWS + 16].astype(BF16)
        pltpu.make_async_copy(out.at[:, cols], gpool_ref.at[:, cols], out_sem).start()
        return 0

    lax.fori_loop(0, 8, pool_grad, 0)

    plane_of = zy // 8
    for t in range(8):
        there = core * 8 + t
        target = (at["x"] * 2 + plane_of, there)
        me = jnp.logical_and(there == zy, plane_of == core)
        src = gp_tx.at[:, pl.ds(pl.multiple_of(there * 256, 256), 256)]
        place = lax.rem(zy, 8)

        @pl.when(me)
        def _():
            pltpu.make_async_copy(src, gp_rx.at[place], gp_recv.at[place]).start()

        @pl.when(jnp.logical_not(me))
        def _():
            send(src, gp_rx.at[place], gp_send.at[t], gp_recv.at[place], target)

    rs_finish(views)
    rs_finish(rs_phase(1))
    rs_finish(rs_phase(2))

    for part in range(3):
        c, b, a = slot(part)
        o = PART_OFF[part]
        gq_ref[o : o + RS_ROWS[part]] = ds[part][c, b, a]
    for i in range(8):
        arrived(gp_rx.at[i], gp_recv.at[i])
        gp_ref[16 * i : 16 * i + 16] = gp_rx[i]
    loss_copy.wait_recv()
    loss_ref[...] = (loss_own[...] + loss_sib[...]) / BATCH

    for copy in pending:
        copy.wait_send()
    for copy in (pool_copy, q_copy, w_copy, loss_copy):
        copy.wait_send()
    for t in range(8):
        for other in range(2):
            chip = core * 8 + t
            me = jnp.logical_and(chip == zy, core == other)

            @pl.when(jnp.logical_not(me))
            def _():
                arrived(p_ref.at[16 * t : 16 * t + 16], pas_send.at[t * 2 + other])

        me = jnp.logical_and(core * 8 + t == zy, plane_of == core)

        @pl.when(jnp.logical_not(me))
        def _():
            arrived(gp_rx.at[0], gp_send.at[t])

    pltpu.make_async_copy(out, gpool_ref, out_sem).wait()


def body(queries, passages, pool_rows, negatives):
    names = jnp.pad(negatives, ((0, 0), (0, 256 - NEGS)))
    vmem = pl.BlockSpec(memory_space=pltpu.VMEM)
    hbm = pl.BlockSpec(memory_space=pl.ANY)
    dma = pltpu.SemaphoreType.DMA
    rs = []
    for rows in RS_ROWS:
        rs += [pltpu.VMEM((2, 4, rows, 256), BF16)] * 2
        rs += [pltpu.VMEM((2, rows, 256), BF16)] * 2
        rs += [pltpu.VMEM((4, 4, rows, 256), BF16)] * 2
        rs += [pltpu.VMEM((4, rows, 256), BF16)] * 2
        rs += [pltpu.VMEM((rows, 128), BF16)] * 2
        rs += [pltpu.VMEM((rows, 256), BF16)] * 2
    loss, gq, gp, gpool = pl.pallas_call(
        kernel,
        out_shape=(
            jax.ShapeDtypeStruct((8, 128), F32),
            jax.ShapeDtypeStruct((128, 256), BF16),
            jax.ShapeDtypeStruct((128, 256), BF16),
            jax.ShapeDtypeStruct((ROWS, D), BF16),
        ),
        in_specs=[vmem, vmem, hbm, vmem],
        out_specs=(vmem, vmem, vmem, hbm),
        scratch_shapes=[
            *[pltpu.VMEM((4, 4, 4, AG_ROWS, 256), BF16)] * 3,
            pltpu.VMEM((2 * ROWS, D), BF16),
            pltpu.VMEM((2 * PLANE, D), BF16),
            pltpu.VMEM((16, 16, 256), BF16),
            pltpu.VMEM((16, D), BF16),
            pltpu.VMEM((2 * ROWS, PLANE), F32),
            pltpu.VMEM((16, PLANE), F32),
            pltpu.VMEM((128, PLANE), jnp.int32),
            pltpu.VMEM((PLANE, 2 * ROWS), BF16),
            pltpu.VMEM((PLANE, 16), BF16),
            pltpu.VMEM((ROWS + 16, 2 * PLANE), BF16),
            pltpu.VMEM((ROWS + 16, PLANE), BF16),
            pltpu.VMEM((PLANE, 128), F32),
            pltpu.VMEM((3, 4, 8, PLANE), F32),
            pltpu.VMEM((8, 128), F32),
            pltpu.VMEM((8, 128), F32),
            pltpu.VMEM((16, D), BF16),
            pltpu.VMEM((8, 16, 256), BF16),
            pltpu.VMEM((ROWS, D), BF16),
            *[pltpu.VMEM((4, 4, 4, rows, 256), BF16) for rows in RS_ROWS],
            *rs,
            dma, dma, dma, dma((36,)), dma((36,)), dma((16,)), dma((16,)), dma, dma,
            dma((12,)), dma((12,)), dma, dma, dma((36,)), dma((36,)), dma((8,)), dma((8,)), dma, dma, dma,
        ],
        compiler_params=pltpu.CompilerParams(
            collective_id=0, has_side_effects=True, vmem_limit_bytes=60 * 1024 * 1024
        ),
    )(queries, passages, pool_rows, names)
    return loss[0, 0], gq, gp, gpool


def solution(mesh):
    placed = (P("dp", "mp"), P("dp", "mp"), P(("dp", "mp"), None), P(("dp", "mp"), None))
    return jax.shard_map(
        body,
        mesh=mesh,
        in_specs=placed,
        out_specs=(P(), P("dp", "mp"), P("dp", "mp"), P(("dp", "mp"), None)),
        check_vma=False,
    )
```

```python
import jax
import jax.numpy as jnp
from jax import lax
from jax.experimental import pallas as pl
from jax.experimental.pallas import tpu as pltpu
from jax.sharding import PartitionSpec as P

MESH = pl.DeviceIdType.MESH
F32 = jnp.float32
BF16 = jnp.bfloat16

D = 4096
NEGS = 31
BATCH = 1024
ROWS = 512
PLANE = 512
SCALE = 1.0 / 64.0
ORDERS = ("xyz", "yzx", "zxy")
PART_OFF = (0, 48, 96)
AG_ROWS = 48
RS_ROWS = (48, 48, 32)
LOW = -1e30


def kernel(
    q_ref, p_ref, pool_ref, neg_ref,
    loss_ref, gq_ref, gp_ref, gpool_ref,
    ag0, ag1, ag2, pool, queries, pas_rx, pas, scores, pscores, names, et, pet, wd, wx, cols_of,
    stats, loss_own, loss_sib, gp_tx, gp_rx, out,
    d0, d1, d2, hl0, hl1, hl2, hr0, hr1, hr2, fl0, fl1, fl2, fr0, fr1, fr2, r10, r11, r12, r20, r21, r22,
    local_sem, pool_send, pool_recv, ag_send, ag_recv, pas_send, pas_recv, q_send, q_recv,
    st_send, st_recv, w_send, w_recv, rs_send, rs_recv, gp_send, gp_recv, loss_send, loss_recv, out_sem,
):
    dp = lax.axis_index("dp")
    mp = lax.axis_index("mp")
    core = lax.rem(dp, 2)
    at = {"x": dp // 2, "y": lax.rem(mp, 4), "z": mp // 4}
    zy = mp
    sib = (at["x"] * 2 + 1 - core, mp)

    def peer(axis, delta):
        there = dict(at)
        there[axis] = lax.rem(at[axis] + delta, 4)
        return (there["x"] * 2 + core, there["z"] * 4 + there["y"])

    def send(src, dst, send_sem, recv_sem, device):
        copy = pltpu.make_async_remote_copy(
            src_ref=src, dst_ref=dst, send_sem=send_sem, recv_sem=recv_sem,
            device_id=device, device_id_type=MESH,
        )
        copy.start()
        return copy

    def arrived(ref, sem):
        pltpu.make_async_copy(ref, ref, sem).wait()

    barrier = pltpu.get_barrier_semaphore()
    for axis in "xyz":
        for delta in (1, 2, 3):
            pl.semaphore_signal(barrier, inc=1, device_id=peer(axis, delta), device_id_type=MESH)
    pl.semaphore_signal(barrier, inc=1, device_id=sib, device_id_type=MESH)

    pending = []
    own_pool = pltpu.make_async_copy(pool_ref, pool.at[0:ROWS], local_sem)
    own_pool.start()

    ags = (ag0, ag1, ag2)

    def slot(part):
        a, b, c = ORDERS[part]
        return at[c], at[b], at[a]

    ids = neg_ref[...]
    high = (ids >> 8).astype(F32)
    low = (ids & 255).astype(F32)
    tile = jnp.concatenate([high, low], axis=0)
    tile = jnp.concatenate([tile, jnp.zeros((16, 128 - NEGS), F32)], axis=1).astype(BF16)
    for s in range(2):
        cols = slice(128 * s, 128 * s + 128)
        for part in range(3):
            c, b, a = slot(part)
            o = PART_OFF[part]
            ags[part][s, c, b, a, 0 : RS_ROWS[part]] = q_ref[o : o + RS_ROWS[part], cols]
        ag2[s, c, b, a, 32:48] = tile
    pl.semaphore_wait(barrier, 10)

    for part in range(3):
        c, b, a = slot(part)
        own = ags[part].at[:, c, b, a]
        for delta in (1, 2, 3):
            k = part * 22 + delta - 1
            pending.append(send(own, own, ag_send.at[k], ag_recv.at[k], peer(ORDERS[part][0], delta)))
    pool_copy = send(pool_ref, pool.at[ROWS : 2 * ROWS], pool_send, pool_recv, sib)

    def third(part, j, view, k):
        axis = ORDERS[part][2]
        pending.append(send(view, view, ag_send.at[k], ag_recv.at[k], peer(axis, 1)))
        pending.append(send(view, view, ag_send.at[k + 1], ag_recv.at[k + 1], peer(axis, 3)))

    for part in range(3):
        c, b, a = slot(part)
        buf = ags[part]
        for delta in (1, 2, 3):
            arrived(buf.at[:, c, b, lax.rem(a + 4 - delta, 4)], ag_recv.at[part * 22 + delta - 1])
        line = buf.at[:, c, b]
        for delta in (1, 2, 3):
            k = part * 22 + 3 + delta - 1
            pending.append(send(line, line, ag_send.at[k], ag_recv.at[k], peer(ORDERS[part][1], delta)))
        third(part, 0, buf.at[0, c, b], part * 22 + 6)
    for part in range(3):
        c, b, a = slot(part)
        buf = ags[part]
        for delta in (1, 2, 3):
            arrived(buf.at[:, c, lax.rem(b + 4 - delta, 4)], ag_recv.at[part * 22 + 3 + delta - 1])
        for j in (1, 2, 3):
            third(part, j, buf.at[0, c, lax.rem(b + j, 4)], part * 22 + 6 + 2 * j)
    for part in range(3):
        c, b, a = slot(part)
        third(part, 0, ags[part].at[1, c], part * 22 + 18)

    for t in range(8):
        for other in range(2):
            chip = core * 8 + t
            target = (at["x"] * 2 + other, chip)
            me = jnp.logical_and(chip == zy, core == other)
            src = p_ref.at[16 * t : 16 * t + 16]
            dst = pas_rx.at[zy]
            k = t * 2 + other

            @pl.when(me)
            def _():
                pltpu.make_async_copy(src, dst, pas_recv.at[zy]).start()

            @pl.when(jnp.logical_not(me))
            def _():
                send(src, dst, pas_send.at[k], pas_recv.at[zy], target)

    for part in range(3):
        c, b, a = slot(part)
        buf = ags[part]
        axis = ORDERS[part][2]
        before, after = lax.rem(c + 3, 4), lax.rem(c + 1, 4)
        for j in range(4):
            bb = lax.rem(b + j, 4)
            k = part * 22 + 6 + 2 * j
            kf = part * 22 + 14 + j
            arrived(buf.at[0, before, bb], ag_recv.at[k])
            arrived(buf.at[0, after, bb], ag_recv.at[k + 1])
            view = buf.at[0, before if j < 2 else after, bb]
            pending.append(send(view, view, ag_send.at[kf], ag_recv.at[kf], peer(axis, 1 if j < 2 else 3)))
    for part in range(3):
        c, b, a = slot(part)
        buf = ags[part]
        axis = ORDERS[part][2]
        before, after = lax.rem(c + 3, 4), lax.rem(c + 1, 4)
        k = part * 22 + 18
        arrived(buf.at[1, before], ag_recv.at[k])
        view = buf.at[1, before, 0:2]
        pending.append(send(view, view, ag_send.at[k + 2], ag_recv.at[k + 2], peer(axis, 1)))
        arrived(buf.at[1, after], ag_recv.at[k + 1])
        view = buf.at[1, after, 2:4]
        pending.append(send(view, view, ag_send.at[k + 3], ag_recv.at[k + 3], peer(axis, 3)))

    contract = (((1,), (1,)), ((), ()))

    def assemble(s):
        def one(i, _):
            z, y = i // 4, lax.rem(i, 4)
            cols = pl.ds(pl.multiple_of(i * 256 + 128 * s, 128), 128)
            for x in range(4):
                where = {"x": x, "y": y, "z": z}
                for part in range(3):
                    aa, bb, cc = ORDERS[part]
                    rows = RS_ROWS[part]
                    start = x * 128 + PART_OFF[part]
                    queries[start : start + rows, cols] = ags[part][s, where[cc], where[bb], where[aa], 0:rows]
            return 0

        lax.fori_loop(0, 16, one, 0)

    def halves(ref, rows, first, count, s):
        return jnp.concatenate(
            [
                ref[rows, pl.ds(pl.multiple_of((first + j) * 256 + 128 * s, 128), 128)]
                for j in range(count)
            ],
            axis=1,
        )

    everything = slice(None)
    plane = slice(0, PLANE)

    def score(s):
        def one(i, _):
            left = halves(pool, everything, 8 * i, 8, s)
            right = halves(queries, plane, 8 * i, 8, s)
            scores[...] += lax.dot_general(left, right, contract, preferred_element_type=F32)
            return 0

        lax.fori_loop(0, 2, one, 0)

    scores[...] = jnp.zeros_like(scores)
    for part in range(3):
        c, b, a = slot(part)
        far = lax.rem(c + 2, 4)
        for j in range(4):
            arrived(ags[part].at[0, far, lax.rem(b + j, 4)], ag_recv.at[part * 22 + 14 + j])
    assemble(0)

    mine = dp * 16 + mp
    theirs = (at["x"] * 2 + 1 - core) * 16 + mp
    sub = lax.broadcasted_iota(jnp.int32, (128, 128), 0)
    for x in range(4):
        pieces = []
        for i in range(16):
            where = {"x": x, "y": i % 4, "z": i // 4}
            aa, bb, cc = ORDERS[2]
            tile = ag2[0, where[cc], where[bb], where[aa], 32:48].astype(F32)
            pieces.append(tile[0:8] * 256.0 + tile[8:16])
        named = jnp.concatenate(pieces, axis=0).T[0:32].astype(jnp.int32)
        owner = named >> 9
        field = ((named >> 7) & 3) * 4
        bit = jnp.where(
            owner == mine, jnp.left_shift(1, field),
            jnp.where(owner == theirs, jnp.left_shift(1, field + 16), 0),
        )
        hi = named & 127
        packed = jnp.zeros((128, 128), jnp.int32)
        for k in range(NEGS):
            packed = packed + jnp.where(sub == hi[k : k + 1], bit[k : k + 1], 0)
        names[:, 128 * x : 128 * x + 128] = packed

    own_pool.wait()
    pool_copy.wait_recv()
    score(0)
    for i in range(16):
        arrived(pas_rx.at[i], pas_recv.at[i])
        pas[:, 256 * i : 256 * i + 256] = pas_rx[i]

    for part in range(3):
        c, b, a = slot(part)
        far = lax.rem(c + 2, 4)
        arrived(ags[part].at[1, far, 0:2], ag_recv.at[part * 22 + 20])
        arrived(ags[part].at[1, far, 2:4], ag_recv.at[part * 22 + 21])
    assemble(1)
    q_copy = send(queries.at[0:PLANE], queries.at[PLANE : 2 * PLANE], q_send, q_recv, sib)
    score(1)
    ps = lax.dot_general(pas[...], queries[0:PLANE, :], contract, preferred_element_type=F32) * SCALE

    lane = lax.broadcasted_iota(jnp.int32, (16, PLANE), 1)
    psub = lax.broadcasted_iota(jnp.int32, (16, PLANE), 0)
    in_plane = core == zy // 8
    first = jnp.where(in_plane, at["x"] * 128 + lax.rem(zy, 8) * 16, -1024)
    same = lane == first + psub
    pos = jnp.sum(jnp.where(same, ps, 0.0), axis=0, keepdims=True)

    def count_of(f):
        return (names[...] >> (4 * f)) & 15

    top = jnp.max(ps, axis=0, keepdims=True)
    for f in range(8):
        s = jnp.where(count_of(f) > 0, scores[128 * f : 128 * f + 128] * SCALE, LOW)
        scores[128 * f : 128 * f + 128] = s
        top = jnp.maximum(top, jnp.max(s, axis=0, keepdims=True))
    pe = jnp.exp(ps - top)
    pscores[...] = pe
    total = jnp.sum(pe, axis=0, keepdims=True)
    for f in range(8):
        e = jnp.exp(scores[128 * f : 128 * f + 128] - top) * count_of(f).astype(F32)
        scores[128 * f : 128 * f + 128] = e
        total = total + jnp.sum(e, axis=0, keepdims=True)
        et[:, 128 * f : 128 * f + 128] = e.T.astype(BF16)
    pet[...] = pe.T.astype(BF16)

    filler = jnp.zeros((5, PLANE), F32)
    within = lax.rem(lax.broadcasted_iota(jnp.int32, (1, PLANE), 1), 128)

    def by_part(values):
        return jnp.where(within < 48, values[0], jnp.where(within < 96, values[1], values[2]))

    def stats_send(n, values):
        tile = jnp.concatenate(list(values) + [filler], axis=0)
        for i, axis in enumerate("xyz"):
            g = at[axis]
            stats[n, i, g] = tile
            for delta in (1, 2, 3):
                k = n * 9 + i * 3 + delta - 1
                ref = stats.at[n, i, g]
                pending.append(send(ref, ref, st_send.at[k], st_recv.at[k], peer(axis, delta)))

    def stats_meet(n):
        sums = {}
        for i, axis in enumerate("xyz"):
            g = at[axis]
            for delta in (1, 2, 3):
                arrived(stats.at[n, i, lax.rem(g + 4 - delta, 4)], st_recv.at[n * 9 + i * 3 + delta - 1])
            parts = [stats[n, i, j] for j in range(4)]
            best = parts[0][0:1]
            for j in range(1, 4):
                best = jnp.maximum(best, parts[j][0:1])
            summed = jnp.zeros_like(best)
            positive = jnp.zeros_like(best)
            for j in range(4):
                summed = summed + parts[j][1:2] * jnp.exp(parts[j][0:1] - best)
                positive = positive + parts[j][2:3]
            sums[axis] = (best, summed, positive)
        return tuple(by_part([sums[ORDERS[part][2 - n]][v] for part in range(3)]) for v in range(3))

    def place_column(index, row):
        wide = jnp.broadcast_to(row, (128, PLANE))
        for x in range(4):
            cols_of[index, 128 * x : 128 * x + 128] = wide[:, 128 * x : 128 * x + 128].T

    stats_send(0, (top, total, pos))

    ds = (d0, d1, d2)

    def back(s):
        def one(i, _):
            right = halves(pool, everything, 2 * i, 2, s)
            pright = halves(pas, everything, 2 * i, 2, s)
            acc = jnp.dot(et[...], right, preferred_element_type=F32)
            acc = (acc + jnp.dot(pet[...], pright, preferred_element_type=F32)).astype(BF16)
            for j in range(2):
                z, y = (2 * i + j) // 4, lax.rem(2 * i + j, 4)
                for x in range(4):
                    where = {"x": x, "y": y, "z": z}
                    for part in range(3):
                        aa, bb, cc = ORDERS[part]
                        o = x * 128 + PART_OFF[part]
                        ds[part][s, where[cc], where[bb], where[aa]] = acc[o : o + RS_ROWS[part], 128 * j : 128 * j + 128]
            return 0

        lax.fori_loop(0, 8, one, 0)

    hls, hrs, fls, frs = (hl0, hl1, hl2), (hr0, hr1, hr2), (fl0, fl1, fl2), (fr0, fr1, fr2)
    r1s, r2s = (r10, r11, r12), (r20, r21, r22)

    def scatter_key(part, s):
        return (part * 2 + s) * 12

    def scatter_start(s):
        for part in range(3):
            c, b, a = slot(part)
            axis = ORDERS[part][2]
            k = scatter_key(part, s)
            d = ds[part]
            far, before, after = lax.rem(c + 2, 4), lax.rem(c + 3, 4), lax.rem(c + 1, 4)
            right, left = peer(axis, 1), peer(axis, 3)
            pending.append(send(d.at[s, far, 0:2], hls[part].at[s], rs_send.at[k], rs_recv.at[k], right))
            pending.append(send(d.at[s, far, 2:4], hrs[part].at[s], rs_send.at[k + 1], rs_recv.at[k + 1], left))
            pending.append(send(d.at[s, after, 2:4], fls[part].at[s, 2:4], rs_send.at[k + 2], rs_recv.at[k + 2], right))
            pending.append(send(d.at[s, before, 0:2], frs[part].at[s, 0:2], rs_send.at[k + 3], rs_recv.at[k + 3], left))

    def factor_rows(part, index, c, b, a):
        x = dict(zip(ORDERS[part], (a, b, c)))["x"]
        return cols_of[index, pl.ds(pl.multiple_of(x * 128 + PART_OFF[part], 16), RS_ROWS[part])]

    def scatter_forward(s):
        for part in range(3):
            c, b, a = slot(part)
            axis = ORDERS[part][2]
            k = scatter_key(part, s)
            d, hl, hr = ds[part], hls[part], hrs[part]
            before, after = lax.rem(c + 3, 4), lax.rem(c + 1, 4)

            def add(i, _, block, base, rx, column):
                bb, aa = i // 4, lax.rem(i, 4)
                own = d[s, block, base + bb, aa].astype(F32) * factor_rows(part, 0, block, base + bb, aa)
                other = rx[s, bb, aa].astype(F32) * factor_rows(part, column, block, base + bb, aa)
                d[s, block, base + bb, aa] = (own + other).astype(BF16)
                return 0

            arrived(hl.at[s], rs_recv.at[k])
            lax.fori_loop(0, 8, lambda i, t: add(i, t, after, 0, hl, 1), 0)
            pending.append(send(
                d.at[s, after, 0:2], fls[part].at[s, 0:2], rs_send.at[k + 4], rs_recv.at[k + 4], peer(axis, 1)
            ))
            arrived(hr.at[s], rs_recv.at[k + 1])
            lax.fori_loop(0, 8, lambda i, t: add(i, t, before, 2, hr, 2), 0)
            pending.append(send(
                d.at[s, before, 2:4], frs[part].at[s, 2:4], rs_send.at[k + 5], rs_recv.at[k + 5], peer(axis, 3)
            ))

    def scatter_second(s):
        for part in range(3):
            c, b, a = slot(part)
            k = scatter_key(part, s)
            d, fl, fr = ds[part], fls[part], frs[part]
            arrived(fl.at[s, 2:4], rs_recv.at[k + 2])
            arrived(fr.at[s, 0:2], rs_recv.at[k + 3])
            arrived(fl.at[s, 0:2], rs_recv.at[k + 4])
            arrived(fr.at[s, 2:4], rs_recv.at[k + 5])

            def low_half(i, _):
                bb, aa = i // 4, lax.rem(i, 4)
                total = d[s, c, bb, aa].astype(F32) * factor_rows(part, 0, c, bb, aa)
                total = total + fr[s, bb, aa].astype(F32) * factor_rows(part, 2, c, bb, aa) + fl[s, bb, aa].astype(F32)
                d[s, c, bb, aa] = (total * factor_rows(part, 3, c, bb, aa)).astype(BF16)
                return 0

            def high_half(i, _):
                bb, aa = i // 4 + 2, lax.rem(i, 4)
                total = d[s, c, bb, aa].astype(F32) * factor_rows(part, 0, c, bb, aa)
                total = total + fl[s, bb, aa].astype(F32) * factor_rows(part, 1, c, bb, aa) + fr[s, bb, aa].astype(F32)
                d[s, c, bb, aa] = (total * factor_rows(part, 3, c, bb, aa)).astype(BF16)
                return 0

            lax.fori_loop(0, 8, low_half, 0)
            lax.fori_loop(0, 8, high_half, 0)
            for delta in (1, 2, 3):
                pending.append(send(
                    d.at[s, c, lax.rem(b + delta, 4)], r1s[part].at[s, delta - 1],
                    rs_send.at[k + 5 + delta], rs_recv.at[k + 5 + delta], peer(ORDERS[part][1], delta),
                ))

    def scatter_third(s):
        for part in range(3):
            c, b, a = slot(part)
            k = scatter_key(part, s)
            d, r1 = ds[part], r1s[part]
            for delta in (1, 2, 3):
                arrived(r1.at[s, delta - 1], rs_recv.at[k + 5 + delta])
            for aa in range(4):
                total = d[s, c, b, aa].astype(F32)
                for j in range(3):
                    total = total + r1[s, j, aa].astype(F32)
                d[s, c, b, aa] = (total * factor_rows(part, 4, c, b, aa)).astype(BF16)
            for delta in (1, 2, 3):
                pending.append(send(
                    d.at[s, c, b, lax.rem(a + delta, 4)], r2s[part].at[s, delta - 1],
                    rs_send.at[k + 8 + delta], rs_recv.at[k + 8 + delta], peer(ORDERS[part][0], delta),
                ))

    def scatter_end(s):
        for part in range(3):
            c, b, a = slot(part)
            k = scatter_key(part, s)
            d, r2 = ds[part], r2s[part]
            total = d[s, c, b, a].astype(F32)
            for delta in (1, 2, 3):
                arrived(r2.at[s, delta - 1], rs_recv.at[k + 8 + delta])
                total = total + r2[s, delta - 1].astype(F32)
            rows = slice(PART_OFF[part], PART_OFF[part] + RS_ROWS[part])
            cols = slice(128 * s, 128 * s + 128)
            total = total * factor_rows(part, 5, c, b, a) - p_ref[rows, cols].astype(F32) * (SCALE / BATCH)
            gq_ref[rows, cols] = total.astype(BF16)

    back(0)
    scatter_start(0)
    back(1)
    scatter_start(1)

    best1, sum1, pos1 = stats_meet(0)
    stats_send(1, (best1, sum1, pos1))
    place_column(0, jnp.exp(top - best1))
    for index, delta in ((1, 3), (2, 1)):
        theirs_top = by_part([
            stats[0, "xyz".index(ORDERS[part][2]), lax.rem(at[ORDERS[part][2]] + delta, 4)][0:1] for part in range(3)
        ])
        place_column(index, jnp.exp(theirs_top - best1))

    scatter_forward(0)
    scatter_forward(1)

    best2, sum2, pos2 = stats_meet(1)
    stats_send(2, (best2, sum2, pos2))
    place_column(3, jnp.exp(best1 - best2))

    scatter_second(0)

    best3, sum3, pos3 = stats_meet(2)
    log_total = best3 + jnp.log(sum3)
    place_column(4, jnp.exp(best2 - best3))
    place_column(5, jnp.exp(best3 - log_total) * (SCALE / BATCH))
    loss_own[...] = jnp.broadcast_to(jnp.sum(log_total - pos3, axis=1, keepdims=True), (8, 128))
    loss_copy = send(loss_own, loss_sib, loss_send, loss_recv, sib)
    factor = jnp.exp(top - log_total) / BATCH

    wp = (pscores[...] * factor - jnp.where(same, 1.0 / BATCH, 0.0)).astype(BF16)
    wx[0:ROWS] = (scores[ROWS : 2 * ROWS] * factor).astype(BF16)
    wx[ROWS : ROWS + 16] = wp
    w_copy = send(wx, wd.at[:, PLANE : 2 * PLANE], w_send, w_recv, sib)
    wd[0:ROWS, 0:PLANE] = (scores[0:ROWS] * factor).astype(BF16)
    wd[ROWS : ROWS + 16, 0:PLANE] = wp

    scatter_second(1)

    q_copy.wait_recv()
    w_copy.wait_recv()

    def pool_grad(i, _):
        cols = pl.ds(pl.multiple_of(i * 512, 512), 512)
        acc = jnp.dot(wd[...], queries[:, cols], preferred_element_type=F32) * SCALE
        out[:, cols] = acc[0:ROWS].astype(BF16)
        gp_tx[:, cols] = acc[ROWS : ROWS + 16].astype(BF16)
        pltpu.make_async_copy(out.at[:, cols], gpool_ref.at[:, cols], out_sem).start()
        return 0

    lax.fori_loop(0, 4, pool_grad, 0)
    scatter_third(0)
    lax.fori_loop(4, 8, pool_grad, 0)
    scatter_third(1)

    plane_of = zy // 8
    for t in range(8):
        there = core * 8 + t
        target = (at["x"] * 2 + plane_of, there)
        me = jnp.logical_and(there == zy, plane_of == core)
        src = gp_tx.at[:, pl.ds(pl.multiple_of(there * 256, 256), 256)]
        place = lax.rem(zy, 8)

        @pl.when(me)
        def _():
            pltpu.make_async_copy(src, gp_rx.at[place], gp_recv.at[place]).start()

        @pl.when(jnp.logical_not(me))
        def _():
            send(src, gp_rx.at[place], gp_send.at[t], gp_recv.at[place], target)

    scatter_end(0)
    scatter_end(1)

    for i in range(8):
        arrived(gp_rx.at[i], gp_recv.at[i])
        gp_ref[16 * i : 16 * i + 16] = gp_rx[i]
    loss_copy.wait_recv()
    loss_ref[...] = (loss_own[...] + loss_sib[...]) / BATCH

    for copy in pending:
        copy.wait_send()
    for copy in (pool_copy, q_copy, w_copy, loss_copy):
        copy.wait_send()
    for t in range(8):
        for other in range(2):
            chip = core * 8 + t
            me = jnp.logical_and(chip == zy, core == other)

            @pl.when(jnp.logical_not(me))
            def _():
                arrived(p_ref.at[16 * t : 16 * t + 16], pas_send.at[t * 2 + other])

        me = jnp.logical_and(core * 8 + t == zy, plane_of == core)

        @pl.when(jnp.logical_not(me))
        def _():
            arrived(gp_rx.at[0], gp_send.at[t])

    pltpu.make_async_copy(out, gpool_ref, out_sem).wait()


def hand_on(loss_in, gq_in, gp_in, gpool_in, loss_out, gq_out, gp_out, gpool_out):
    gpool_out[...] = gpool_in[...]

    @pl.when(pl.program_id(0) == 0)
    def _():
        loss_out[0, 0] = loss_in[0, 0]
        gq_out[...] = gq_in[...]
        gp_out[...] = gp_in[...]


def body(queries, passages, pool_rows, negatives):
    vmem = pl.BlockSpec(memory_space=pltpu.VMEM)
    smem = pl.BlockSpec(memory_space=pltpu.SMEM)
    hbm = pl.BlockSpec(memory_space=pl.ANY)
    dma = pltpu.SemaphoreType.DMA
    pieces = jax.ShapeDtypeStruct((128, 256), BF16)
    rows_out = jax.ShapeDtypeStruct((ROWS, D), BF16)
    loss, gq, gp, gpool = pl.pallas_call(
        kernel,
        out_shape=(jax.ShapeDtypeStruct((8, 128), F32), pieces, pieces, rows_out),
        in_specs=[vmem, vmem, hbm, vmem],
        out_specs=(vmem, vmem, vmem, hbm),
        scratch_shapes=[
            *[pltpu.VMEM((2, 4, 4, 4, AG_ROWS, 128), BF16)] * 3,
            pltpu.VMEM((2 * ROWS, D), BF16),
            pltpu.VMEM((2 * PLANE, D), BF16),
            pltpu.VMEM((16, 16, 256), BF16),
            pltpu.VMEM((16, D), BF16),
            pltpu.VMEM((2 * ROWS, PLANE), F32),
            pltpu.VMEM((16, PLANE), F32),
            pltpu.VMEM((128, PLANE), jnp.int32),
            pltpu.VMEM((PLANE, 2 * ROWS), BF16),
            pltpu.VMEM((PLANE, 16), BF16),
            pltpu.VMEM((ROWS + 16, 2 * PLANE), BF16),
            pltpu.VMEM((ROWS + 16, PLANE), BF16),
            pltpu.VMEM((6, PLANE, 128), F32),
            pltpu.VMEM((3, 3, 4, 8, PLANE), F32),
            pltpu.VMEM((8, 128), F32),
            pltpu.VMEM((8, 128), F32),
            pltpu.VMEM((16, D), BF16),
            pltpu.VMEM((8, 16, 256), BF16),
            pltpu.VMEM((ROWS, D), BF16),
            *[pltpu.VMEM((2, 4, 4, 4, rows, 128), BF16) for rows in RS_ROWS],
            *[pltpu.VMEM((2, 2, 4, rows, 128), BF16) for rows in RS_ROWS],
            *[pltpu.VMEM((2, 2, 4, rows, 128), BF16) for rows in RS_ROWS],
            *[pltpu.VMEM((2, 4, 4, rows, 128), BF16) for rows in RS_ROWS],
            *[pltpu.VMEM((2, 4, 4, rows, 128), BF16) for rows in RS_ROWS],
            *[pltpu.VMEM((2, 3, 4, rows, 128), BF16) for rows in RS_ROWS],
            *[pltpu.VMEM((2, 3, rows, 128), BF16) for rows in RS_ROWS],
            dma, dma, dma, dma((66,)), dma((66,)), dma((16,)), dma((16,)), dma, dma,
            dma((27,)), dma((27,)), dma, dma, dma((72,)), dma((72,)), dma((8,)), dma((8,)), dma, dma, dma,
        ],
        compiler_params=pltpu.CompilerParams(
            collective_id=0, has_side_effects=True, vmem_limit_bytes=60 * 1024 * 1024
        ),
    )(queries, passages, pool_rows, negatives)
    small = pl.BlockSpec((128, 256), lambda i: (0, 0))
    large = pl.BlockSpec((ROWS // 8, D), lambda i: (i, 0))
    loss, gq, gp, gpool = pl.pallas_call(
        hand_on,
        grid=(8,),
        out_shape=(jax.ShapeDtypeStruct((1, 1), F32), pieces, pieces, rows_out),
        in_specs=[smem, small, small, large],
        out_specs=(smem, small, small, large),
        compiler_params=pltpu.CompilerParams(vmem_limit_bytes=60 * 1024 * 1024),
    )(loss, gq, gp, gpool)
    return loss[0, 0], gq, gp, gpool


def solution(mesh):
    placed = (P("dp", "mp"), P("dp", "mp"), P(("dp", "mp"), None), P(("dp", "mp"), None))
    return jax.shard_map(
        body,
        mesh=mesh,
        in_specs=placed,
        out_specs=(P(), P("dp", "mp"), P("dp", "mp"), P(("dp", "mp"), None)),
        check_vma=False,
    )
```

```python
import jax
import jax.numpy as jnp
from jax import lax
from jax.experimental import pallas as pl
from jax.experimental.pallas import tpu as pltpu
from jax.sharding import PartitionSpec as P

MESH = pl.DeviceIdType.MESH
F32 = jnp.float32
BF16 = jnp.bfloat16

D = 4096
NEGS = 31
BATCH = 1024
ROWS = 512
PLANE = 512
SCALE = 1.0 / 64.0
ORDERS = ("xyz", "yzx", "zxy")
HALF = 256
AG_ROWS = 48
RS_ROWS = (48, 48, 32)
UNITS = (((0, 48, 0, 0),), ((0, 48, 1, 0),), ((48, 16, 0, 0), (48, 16, 1, 16)))
LOW = -1e30


def kernel(
    q_hbm, p_hbm, pool_ref, neg_hbm,
    loss_ref, gq_ref, gp_ref, gpool_ref,
    q_ref, p_ref, neg_ref, in_sem, ag0, ag1, ag2, pool, queries, pas_rx, scores, names, et, pet, wd, wx, cols_of,
    stats, loss_own, loss_sib, gp_tx, gp_rx,
    d0, d1, d2, hl0, hl1, hl2, hr0, hr1, hr2, fl0, fl1, fl2, fr0, fr1, fr2, r10, r11, r12, r20, r21, r22,
    local_sem, pool_send, pool_recv, ag_send, ag_recv, pas_send, pas_recv, q_send, q_recv,
    st_send, st_recv, w_send, w_recv, rs_send, rs_recv, gp_send, gp_recv, loss_send, loss_recv,
):
    dp = lax.axis_index("dp")
    mp = lax.axis_index("mp")
    core = lax.rem(dp, 2)
    at = {"x": dp // 2, "y": lax.rem(mp, 4), "z": mp // 4}
    zy = mp
    sib = (at["x"] * 2 + 1 - core, mp)

    def peer(axis, delta):
        there = dict(at)
        there[axis] = lax.rem(at[axis] + delta, 4)
        return (there["x"] * 2 + core, there["z"] * 4 + there["y"])

    def send(src, dst, send_sem, recv_sem, device):
        copy = pltpu.make_async_remote_copy(
            src_ref=src, dst_ref=dst, send_sem=send_sem, recv_sem=recv_sem,
            device_id=device, device_id_type=MESH,
        )
        copy.start()
        return copy

    def arrived(ref, sem):
        pltpu.make_async_copy(ref, ref, sem).wait()

    barrier = pltpu.get_barrier_semaphore()
    for axis in "xyz":
        for delta in (1, 2, 3):
            pl.semaphore_signal(barrier, inc=1, device_id=peer(axis, delta), device_id_type=MESH)
    pl.semaphore_signal(barrier, inc=1, device_id=sib, device_id_type=MESH)

    pending = []
    inputs = [
        pltpu.make_async_copy(src, dst, in_sem.at[i])
        for i, (src, dst) in enumerate(((q_hbm, q_ref), (neg_hbm, neg_ref), (p_hbm, p_ref)))
    ]
    for copy in inputs:
        copy.start()
    own_pool = pltpu.make_async_copy(pool_ref, pool.at[0:ROWS], local_sem)
    own_pool.start()

    ags = (ag0, ag1, ag2)

    def slot(part):
        a, b, c = ORDERS[part]
        return at[c], at[b], at[a]

    for copy in inputs:
        copy.wait()
    ids = neg_ref[...]
    high = (ids >> 8).astype(F32)
    low = (ids & 255).astype(F32)
    tile = jnp.concatenate([high, low], axis=0)
    tile = jnp.concatenate([tile, jnp.zeros((16, 128 - NEGS), F32)], axis=1).astype(BF16)
    for s in range(2):
        for part in range(3):
            c, b, a = slot(part)
            for row, rows, h, o in UNITS[part]:
                piece = q_ref[64 * s + row : 64 * s + row + rows, 128 * h : 128 * h + 128]
                ags[part][s, c, b, a, o : o + rows] = piece
        c, b, a = slot(2)
        ag2[s, c, b, a, 32:48] = tile
    pl.semaphore_wait(barrier, 10)

    for part in range(3):
        c, b, a = slot(part)
        own = ags[part].at[:, c, b, a]
        for delta in (1, 2, 3):
            k = part * 25 + delta - 1
            pending.append(send(own, own, ag_send.at[k], ag_recv.at[k], peer(ORDERS[part][0], delta)))
    pool_copy = send(pool_ref, pool.at[ROWS : 2 * ROWS], pool_send, pool_recv, sib)

    def third(part, view, k):
        axis = ORDERS[part][2]
        pending.append(send(view, view, ag_send.at[k], ag_recv.at[k], peer(axis, 1)))
        pending.append(send(view, view, ag_send.at[k + 1], ag_recv.at[k + 1], peer(axis, 3)))

    def second(part, s):
        c, b, a = slot(part)
        line = ags[part].at[s, c, b]
        for delta in (1, 2, 3):
            k = part * 25 + 3 + 3 * s + delta - 1
            pending.append(send(line, line, ag_send.at[k], ag_recv.at[k], peer(ORDERS[part][1], delta)))

    def second_arrived(part, s):
        c, b, a = slot(part)
        for delta in (1, 2, 3):
            arrived(ags[part].at[s, c, lax.rem(b + 4 - delta, 4)], ag_recv.at[part * 25 + 3 + 3 * s + delta - 1])

    for part in range(3):
        c, b, a = slot(part)
        buf = ags[part]
        for delta in (1, 2, 3):
            arrived(buf.at[:, c, b, lax.rem(a + 4 - delta, 4)], ag_recv.at[part * 25 + delta - 1])
        second(part, 0)
        third(part, buf.at[0, c, b], part * 25 + 9)
    for part in range(3):
        second(part, 1)
    for part in range(3):
        c, b, a = slot(part)
        buf = ags[part]
        second_arrived(part, 0)
        for j in (1, 2, 3):
            third(part, buf.at[0, c, lax.rem(b + j, 4)], part * 25 + 9 + 2 * j)

    for t in range(8):
        for other in range(2):
            chip = core * 8 + t
            target = (at["x"] * 2 + other, chip)
            me = jnp.logical_and(chip == zy, core == other)
            src = p_ref.at[16 * t : 16 * t + 16]
            dst = pas_rx.at[zy]
            k = t * 2 + other

            @pl.when(me)
            def _():
                pltpu.make_async_copy(src, dst, pas_recv.at[zy]).start()

            @pl.when(jnp.logical_not(me))
            def _():
                send(src, dst, pas_send.at[k], pas_recv.at[zy], target)

    for part in range(3):
        c, b, a = slot(part)
        buf = ags[part]
        axis = ORDERS[part][2]
        before, after = lax.rem(c + 3, 4), lax.rem(c + 1, 4)
        for j in range(4):
            bb = lax.rem(b + j, 4)
            k = part * 25 + 9 + 2 * j
            kf = part * 25 + 17 + j
            arrived(buf.at[0, before, bb], ag_recv.at[k])
            arrived(buf.at[0, after, bb], ag_recv.at[k + 1])
            view = buf.at[0, before if j < 2 else after, bb]
            pending.append(send(view, view, ag_send.at[kf], ag_recv.at[kf], peer(axis, 1 if j < 2 else 3)))
    for part in range(3):
        c, b, a = slot(part)
        second_arrived(part, 1)
        third(part, ags[part].at[1, c], part * 25 + 21)

    def forward_last():
        for part in range(3):
            c, b, a = slot(part)
            buf = ags[part]
            axis = ORDERS[part][2]
            before, after = lax.rem(c + 3, 4), lax.rem(c + 1, 4)
            k = part * 25 + 21
            arrived(buf.at[1, before], ag_recv.at[k])
            view = buf.at[1, before, 0:2]
            pending.append(send(view, view, ag_send.at[k + 2], ag_recv.at[k + 2], peer(axis, 1)))
            arrived(buf.at[1, after], ag_recv.at[k + 1])
            view = buf.at[1, after, 2:4]
            pending.append(send(view, view, ag_send.at[k + 3], ag_recv.at[k + 3], peer(axis, 3)))

    contract = (((1,), (1,)), ((), ()))

    def assemble(s):
        def one(i, _):
            z, y = i // 4, lax.rem(i, 4)
            for x in range(4):
                where = {"x": x, "y": y, "z": z}
                for part in range(3):
                    aa, bb, cc = ORDERS[part]
                    for row, rows, h, o in UNITS[part]:
                        start = s * HALF + x * 64 + row
                        cols = pl.ds(pl.multiple_of(i * 256 + 128 * h, 128), 128)
                        piece = ags[part][s, where[cc], where[bb], where[aa], o : o + rows]
                        queries[start : start + rows, cols] = piece
            return 0

        lax.fori_loop(0, 16, one, 0)

    mine = dp * 16 + mp
    theirs = (at["x"] * 2 + 1 - core) * 16 + mp
    sub = lax.broadcasted_iota(jnp.int32, (128, 128), 0)

    def find_names(s):
        for pair in range(2):
            pieces = []
            for x in (2 * pair, 2 * pair + 1):
                for i in range(8 * s, 8 * s + 8):
                    where = {"x": x, "y": i % 4, "z": i // 4}
                    aa, bb, cc = ORDERS[2]
                    tile = ag2[0, where[cc], where[bb], where[aa], 32:48].astype(F32)
                    pieces.append(tile[0:8] * 256.0 + tile[8:16])
            named = jnp.concatenate(pieces, axis=0).T[0:32].astype(jnp.int32)
            owner = named >> 9
            field = ((named >> 7) & 3) * 4
            bit = jnp.where(
                owner == mine, jnp.left_shift(1, field),
                jnp.where(owner == theirs, jnp.left_shift(1, field + 16), 0),
            )
            hi = named & 127
            packed = jnp.zeros((128, 128), jnp.int32)
            for k in range(NEGS):
                packed = packed + jnp.where(sub == hi[k : k + 1], bit[k : k + 1], 0)
            names[s, :, 128 * pair : 128 * pair + 128] = packed

    def score(s):
        rows = slice(s * HALF, s * HALF + HALF)

        def one(i, _):
            cols = pl.ds(pl.multiple_of(i * 2048, 2048), 2048)
            scores[s] += lax.dot_general(pool[:, cols], queries[rows, cols], contract, preferred_element_type=F32)
            return 0

        scores[s] = jnp.zeros((2 * ROWS + 16, HALF), F32)
        lax.fori_loop(0, 2, one, 0)

    lane = lax.broadcasted_iota(jnp.int32, (16, HALF), 1)
    psub = lax.broadcasted_iota(jnp.int32, (16, HALF), 0)
    in_plane = core == zy // 8
    row128 = lax.rem(zy, 8) * 16

    def same_of(s):
        held = jnp.logical_and(in_plane, row128 // 64 == s)
        first = jnp.where(held, at["x"] * 64 + lax.rem(row128, 64), -1024)
        return lane == first + psub

    def soften(s):
        def count_of(f):
            return (names[s] >> (4 * f)) & 15

        ps = scores[s, 2 * ROWS : 2 * ROWS + 16] * SCALE
        pos = jnp.sum(jnp.where(same_of(s), ps, 0.0), axis=0, keepdims=True)
        top = jnp.max(ps, axis=0, keepdims=True)
        for f in range(8):
            v = jnp.where(count_of(f) > 0, scores[s, 128 * f : 128 * f + 128] * SCALE, LOW)
            scores[s, 128 * f : 128 * f + 128] = v
            top = jnp.maximum(top, jnp.max(v, axis=0, keepdims=True))
        pe = jnp.exp(ps - top)
        scores[s, 2 * ROWS : 2 * ROWS + 16] = pe
        total = jnp.sum(pe, axis=0, keepdims=True)
        for f in range(8):
            e = jnp.exp(scores[s, 128 * f : 128 * f + 128] - top) * count_of(f).astype(F32)
            scores[s, 128 * f : 128 * f + 128] = e
            total = total + jnp.sum(e, axis=0, keepdims=True)
            et[s, :, 128 * f : 128 * f + 128] = e.T.astype(BF16)
        pet[s] = pe.T.astype(BF16)
        return top, total, pos

    filler = jnp.zeros((5, HALF), F32)

    def stats_send(s, n, tiles):
        for part in range(3):
            axis = ORDERS[part][2 - n]
            g = at[axis]
            stats[s, n, part, g] = jnp.concatenate(list(tiles[part]) + [filler], axis=0)
            ref = stats.at[s, n, part, g]
            for delta in (1, 2, 3):
                k = ((s * 3 + n) * 3 + part) * 3 + delta - 1
                pending.append(send(ref, ref, st_send.at[k], st_recv.at[k], peer(axis, delta)))

    def stats_meet(s, n):
        met = []
        for part in range(3):
            g = at[ORDERS[part][2 - n]]
            for delta in (1, 2, 3):
                k = ((s * 3 + n) * 3 + part) * 3 + delta - 1
                arrived(stats.at[s, n, part, lax.rem(g + 4 - delta, 4)], st_recv.at[k])
            tiles = [stats[s, n, part, j] for j in range(4)]
            best = tiles[0][0:1]
            for j in range(1, 4):
                best = jnp.maximum(best, tiles[j][0:1])
            summed = jnp.zeros_like(best)
            positive = jnp.zeros_like(best)
            for j in range(4):
                summed = summed + tiles[j][1:2] * jnp.exp(tiles[j][0:1] - best)
                positive = positive + tiles[j][2:3]
            met.append((best, summed, positive))
        return met

    third_part = lax.rem(lax.broadcasted_iota(jnp.int32, (1, HALF), 1), 64) >= 48

    def place_column(s, index, rows):
        for table, row in enumerate((jnp.where(third_part, rows[2], rows[0]), rows[1])):
            wide = jnp.broadcast_to(row, (128, HALF))
            for x in range(2):
                cols_of[s, index, table, 128 * x : 128 * x + 128] = wide[:, 128 * x : 128 * x + 128].T

    ds = (d0, d1, d2)

    def back(s):
        wide = 8

        def one(i, _):
            cols = pl.ds(pl.multiple_of(i * (256 * wide), 256 * wide), 256 * wide)
            acc = jnp.dot(et[s], pool[0 : 2 * ROWS, cols], preferred_element_type=F32)
            acc = (acc + jnp.dot(pet[s], pool[2 * ROWS : 2 * ROWS + 16, cols], preferred_element_type=F32)).astype(BF16)
            for j in range(wide):
                z, y = (i * wide + j) // 4, lax.rem(i * wide + j, 4)
                for x in range(4):
                    where = {"x": x, "y": y, "z": z}
                    for part in range(3):
                        aa, bb, cc = ORDERS[part]
                        for row, rows, h, o in UNITS[part]:
                            left = 256 * j + 128 * h
                            piece = acc[x * 64 + row : x * 64 + row + rows, left : left + 128]
                            ds[part][s, where[cc], where[bb], where[aa], o : o + rows] = piece
            return 0

        lax.fori_loop(0, 16 // wide, one, 0)

    hls, hrs, fls, frs = (hl0, hl1, hl2), (hr0, hr1, hr2), (fl0, fl1, fl2), (fr0, fr1, fr2)
    r1s, r2s = (r10, r11, r12), (r20, r21, r22)

    def scatter_key(part, s):
        return (part * 2 + s) * 12

    def scatter_start(s):
        for part in range(3):
            c, b, a = slot(part)
            axis = ORDERS[part][2]
            k = scatter_key(part, s)
            d = ds[part]
            far, before, after = lax.rem(c + 2, 4), lax.rem(c + 3, 4), lax.rem(c + 1, 4)
            right, left = peer(axis, 1), peer(axis, 3)
            pending.append(send(d.at[s, far, 0:2], hls[part].at[s], rs_send.at[k], rs_recv.at[k], right))
            pending.append(send(d.at[s, far, 2:4], hrs[part].at[s], rs_send.at[k + 1], rs_recv.at[k + 1], left))
            pending.append(send(d.at[s, after, 2:4], fls[part].at[s, 2:4], rs_send.at[k + 2], rs_recv.at[k + 2], right))
            pending.append(send(d.at[s, before, 0:2], frs[part].at[s, 0:2], rs_send.at[k + 3], rs_recv.at[k + 3], left))

    def factor_rows(part, s, index, c, b, a):
        x = dict(zip(ORDERS[part], (a, b, c)))["x"]
        if part < 2:
            return cols_of[s, index, part, pl.ds(pl.multiple_of(x * 64, 16), 48)]
        v = cols_of[s, index, 0, pl.ds(pl.multiple_of(x * 64 + 48, 16), 16)]
        return jnp.concatenate([v, v], axis=0)

    def scatter_forward(s):
        for part in range(3):
            c, b, a = slot(part)
            axis = ORDERS[part][2]
            k = scatter_key(part, s)
            d, hl, hr = ds[part], hls[part], hrs[part]
            before, after = lax.rem(c + 3, 4), lax.rem(c + 1, 4)

            def add(i, _, block, base, rx, column):
                bb, aa = i // 4, lax.rem(i, 4)
                own = d[s, block, base + bb, aa].astype(F32) * factor_rows(part, s, 0, block, base + bb, aa)
                other = rx[s, bb, aa].astype(F32) * factor_rows(part, s, column, block, base + bb, aa)
                d[s, block, base + bb, aa] = (own + other).astype(BF16)
                return 0

            arrived(hl.at[s], rs_recv.at[k])
            lax.fori_loop(0, 8, lambda i, t: add(i, t, after, 0, hl, 1), 0)
            pending.append(send(
                d.at[s, after, 0:2], fls[part].at[s, 0:2], rs_send.at[k + 4], rs_recv.at[k + 4], peer(axis, 1)
            ))
            arrived(hr.at[s], rs_recv.at[k + 1])
            lax.fori_loop(0, 8, lambda i, t: add(i, t, before, 2, hr, 2), 0)
            pending.append(send(
                d.at[s, before, 2:4], frs[part].at[s, 2:4], rs_send.at[k + 5], rs_recv.at[k + 5], peer(axis, 3)
            ))

    def scatter_second(s):
        for part in range(3):
            c, b, a = slot(part)
            k = scatter_key(part, s)
            d, fl, fr = ds[part], fls[part], frs[part]
            arrived(fl.at[s, 2:4], rs_recv.at[k + 2])
            arrived(fr.at[s, 0:2], rs_recv.at[k + 3])
            arrived(fl.at[s, 0:2], rs_recv.at[k + 4])
            arrived(fr.at[s, 2:4], rs_recv.at[k + 5])

            def low_half(i, _):
                bb, aa = i // 4, lax.rem(i, 4)
                total = d[s, c, bb, aa].astype(F32) * factor_rows(part, s, 0, c, bb, aa)
                total = total + fr[s, bb, aa].astype(F32) * factor_rows(part, s, 2, c, bb, aa) + fl[s, bb, aa].astype(F32)
                d[s, c, bb, aa] = (total * factor_rows(part, s, 3, c, bb, aa)).astype(BF16)
                return 0

            def high_half(i, _):
                bb, aa = i // 4 + 2, lax.rem(i, 4)
                total = d[s, c, bb, aa].astype(F32) * factor_rows(part, s, 0, c, bb, aa)
                total = total + fl[s, bb, aa].astype(F32) * factor_rows(part, s, 1, c, bb, aa) + fr[s, bb, aa].astype(F32)
                d[s, c, bb, aa] = (total * factor_rows(part, s, 3, c, bb, aa)).astype(BF16)
                return 0

            lax.fori_loop(0, 8, low_half, 0)
            lax.fori_loop(0, 8, high_half, 0)
            for delta in (1, 2, 3):
                pending.append(send(
                    d.at[s, c, lax.rem(b + delta, 4)], r1s[part].at[s, delta - 1],
                    rs_send.at[k + 5 + delta], rs_recv.at[k + 5 + delta], peer(ORDERS[part][1], delta),
                ))

    def scatter_third(s):
        for part in range(3):
            c, b, a = slot(part)
            k = scatter_key(part, s)
            d, r1 = ds[part], r1s[part]
            for delta in (1, 2, 3):
                arrived(r1.at[s, delta - 1], rs_recv.at[k + 5 + delta])
            for aa in range(4):
                total = d[s, c, b, aa].astype(F32)
                for j in range(3):
                    total = total + r1[s, j, aa].astype(F32)
                d[s, c, b, aa] = (total * factor_rows(part, s, 4, c, b, aa)).astype(BF16)
            for delta in (1, 2, 3):
                pending.append(send(
                    d.at[s, c, b, lax.rem(a + delta, 4)], r2s[part].at[s, delta - 1],
                    rs_send.at[k + 8 + delta], rs_recv.at[k + 8 + delta], peer(ORDERS[part][0], delta),
                ))

    def scatter_end(s):
        for part in range(3):
            c, b, a = slot(part)
            k = scatter_key(part, s)
            d, r2 = ds[part], r2s[part]
            total = d[s, c, b, a].astype(F32)
            for delta in (1, 2, 3):
                arrived(r2.at[s, delta - 1], rs_recv.at[k + 8 + delta])
                total = total + r2[s, delta - 1].astype(F32)
            total = total * factor_rows(part, s, 5, c, b, a)
            for row, rows, h, o in UNITS[part]:
                there = (slice(64 * s + row, 64 * s + row + rows), slice(128 * h, 128 * h + 128))
                gq_ref[there] = (total[o : o + rows] - p_ref[there].astype(F32) * (SCALE / BATCH)).astype(BF16)

    def first_factors(s, top, met):
        best = [met[part][0] for part in range(3)]
        place_column(s, 0, [jnp.exp(top - best[part]) for part in range(3)])
        for index, delta in ((1, 3), (2, 1)):
            rows = []
            for part in range(3):
                there = lax.rem(at[ORDERS[part][2]] + delta, 4)
                rows.append(jnp.exp(stats[s, 0, part, there][0:1] - best[part]))
            place_column(s, index, rows)

    def next_factors(s, index, met, wider):
        place_column(s, index, [jnp.exp(met[part][0] - wider[part][0]) for part in range(3)])

    def finish_stats(s, met, top):
        best, summed, positive = met[0]
        log_total = best + jnp.log(summed)
        place_column(s, 5, [jnp.exp(best - log_total) * (SCALE / BATCH)] * 3)
        return jnp.exp(top - log_total) / BATCH, jnp.sum(log_total - positive, axis=1, keepdims=True)

    def weigh(s, factor):
        own = slice(s * HALF, s * HALF + HALF)
        wp = scores[s, 2 * ROWS : 2 * ROWS + 16] * factor - jnp.where(same_of(s), 1.0 / BATCH, 0.0)
        wp = wp.astype(BF16)
        wx[0:ROWS, own] = (scores[s, ROWS : 2 * ROWS] * factor).astype(BF16)
        wx[ROWS : ROWS + 16, own] = wp
        wd[0:ROWS, own] = (scores[s, 0:ROWS] * factor).astype(BF16)
        wd[ROWS : ROWS + 16, own] = wp

    for part in range(3):
        c, b, a = slot(part)
        far = lax.rem(c + 2, 4)
        for j in range(4):
            arrived(ags[part].at[0, far, lax.rem(b + j, 4)], ag_recv.at[part * 25 + 17 + j])
    assemble(0)
    find_names(0)
    own_pool.wait()
    arrived(pool.at[ROWS : 2 * ROWS], pool_recv)
    for i in range(16):
        arrived(pas_rx.at[i], pas_recv.at[i])
        pool[2 * ROWS : 2 * ROWS + 16, 256 * i : 256 * i + 256] = pas_rx[i]
    score(0)
    forward_last()
    top_a, total_a, pos_a = soften(0)
    stats_send(0, 0, [(top_a, total_a, pos_a)] * 3)
    back(0)
    scatter_start(0)

    find_names(1)
    for part in range(3):
        c, b, a = slot(part)
        far = lax.rem(c + 2, 4)
        arrived(ags[part].at[1, far, 0:2], ag_recv.at[part * 25 + 23])
        arrived(ags[part].at[1, far, 2:4], ag_recv.at[part * 25 + 24])
    assemble(1)
    q_copy = send(queries.at[0:PLANE], queries.at[PLANE : 2 * PLANE], q_send, q_recv, sib)
    score(1)
    met_a1 = stats_meet(0, 0)
    stats_send(0, 1, met_a1)
    first_factors(0, top_a, met_a1)
    scatter_forward(0)
    top_b, total_b, pos_b = soften(1)
    stats_send(1, 0, [(top_b, total_b, pos_b)] * 3)
    back(1)
    scatter_start(1)

    met_a2 = stats_meet(0, 1)
    stats_send(0, 2, met_a2)
    next_factors(0, 3, met_a1, met_a2)
    scatter_second(0)
    met_b1 = stats_meet(1, 0)
    stats_send(1, 1, met_b1)
    first_factors(1, top_b, met_b1)
    scatter_forward(1)
    met_a3 = stats_meet(0, 2)
    next_factors(0, 4, met_a2, met_a3)
    factor_a, loss_a = finish_stats(0, met_a3, top_a)
    scatter_third(0)
    met_b2 = stats_meet(1, 1)
    stats_send(1, 2, met_b2)
    next_factors(1, 3, met_b1, met_b2)
    weigh(0, factor_a)
    scatter_second(1)
    met_b3 = stats_meet(1, 2)
    next_factors(1, 4, met_b2, met_b3)
    factor_b, loss_b = finish_stats(1, met_b3, top_b)
    weigh(1, factor_b)
    w_copy = send(wx, wd.at[:, PLANE : 2 * PLANE], w_send, w_recv, sib)
    loss_own[...] = jnp.broadcast_to(loss_a + loss_b, (8, 128))
    loss_copy = send(loss_own, loss_sib, loss_send, loss_recv, sib)

    arrived(queries.at[PLANE : 2 * PLANE], q_recv)
    arrived(wx, w_recv)

    def pool_grad(i, _):
        cols = pl.ds(pl.multiple_of(i * 512, 512), 512)
        acc = jnp.dot(wd[...], queries[:, cols], preferred_element_type=F32) * SCALE
        gpool_ref[:, cols] = acc[0:ROWS].astype(BF16)
        gp_tx[:, cols] = acc[ROWS : ROWS + 16].astype(BF16)
        return 0

    lax.fori_loop(0, 4, pool_grad, 0)
    scatter_third(1)
    lax.fori_loop(4, 8, pool_grad, 0)

    plane_of = zy // 8
    for t in range(8):
        there = core * 8 + t
        target = (at["x"] * 2 + plane_of, there)
        me = jnp.logical_and(there == zy, plane_of == core)
        src = gp_tx.at[:, pl.ds(pl.multiple_of(there * 256, 256), 256)]
        place = lax.rem(zy, 8)

        @pl.when(me)
        def _():
            pltpu.make_async_copy(src, gp_rx.at[place], gp_recv.at[place]).start()

        @pl.when(jnp.logical_not(me))
        def _():
            send(src, gp_rx.at[place], gp_send.at[t], gp_recv.at[place], target)

    scatter_end(0)
    scatter_end(1)

    for i in range(8):
        arrived(gp_rx.at[i], gp_recv.at[i])
        gp_ref[16 * i : 16 * i + 16] = gp_rx[i]
    arrived(loss_sib, loss_recv)
    loss_ref[...] = (loss_own[...] + loss_sib[...]) / BATCH

    for copy in pending:
        copy.wait_send()
    for copy in (pool_copy, q_copy, w_copy, loss_copy):
        copy.wait_send()
    for t in range(8):
        for other in range(2):
            chip = core * 8 + t
            me = jnp.logical_and(chip == zy, core == other)

            @pl.when(jnp.logical_not(me))
            def _():
                arrived(p_ref.at[16 * t : 16 * t + 16], pas_send.at[t * 2 + other])

        me = jnp.logical_and(core * 8 + t == zy, plane_of == core)

        @pl.when(jnp.logical_not(me))
        def _():
            arrived(gp_rx.at[0], gp_send.at[t])


def hand_on(loss_in, gq_in, gp_in, gpool_in, loss_out, gq_out, gp_out, gpool_out, sem):
    copies = [
        pltpu.make_async_copy(src, dst, sem.at[i])
        for i, (src, dst) in enumerate(((gpool_in, gpool_out), (gq_in, gq_out), (gp_in, gp_out)))
    ]
    for copy in copies:
        copy.start()
    loss_out[0, 0] = loss_in[0, 0]
    for copy in copies:
        copy.wait()


def body(queries, passages, pool_rows, negatives):
    vmem = pl.BlockSpec(memory_space=pltpu.VMEM)
    smem = pl.BlockSpec(memory_space=pltpu.SMEM)
    hbm = pl.BlockSpec(memory_space=pltpu.HBM)
    dma = pltpu.SemaphoreType.DMA
    pieces = jax.ShapeDtypeStruct((128, 256), BF16)
    rows_out = jax.ShapeDtypeStruct((ROWS, D), BF16)
    loss, gq, gp, gpool = pl.pallas_call(
        kernel,
        out_shape=(jax.ShapeDtypeStruct((8, 128), F32), pieces, pieces, rows_out),
        in_specs=[hbm, hbm, hbm, hbm],
        out_specs=(vmem, vmem, vmem, vmem),
        scratch_shapes=[
            pltpu.VMEM((128, 256), BF16),
            pltpu.VMEM((128, 256), BF16),
            pltpu.VMEM((8, NEGS), jnp.int32),
            dma((3,)),
            *[pltpu.VMEM((2, 4, 4, 4, AG_ROWS, 128), BF16)] * 3,
            pltpu.VMEM((2 * ROWS + 16, D), BF16),
            pltpu.VMEM((2 * PLANE, D), BF16),
            pltpu.VMEM((16, 16, 256), BF16),
            pltpu.VMEM((2, 2 * ROWS + 16, HALF), F32),
            pltpu.VMEM((2, 128, HALF), jnp.int32),
            pltpu.VMEM((2, HALF, 2 * ROWS), BF16),
            pltpu.VMEM((2, HALF, 16), BF16),
            pltpu.VMEM((ROWS + 16, 2 * PLANE), BF16),
            pltpu.VMEM((ROWS + 16, PLANE), BF16),
            pltpu.VMEM((2, 6, 2, HALF, 128), F32),
            pltpu.VMEM((2, 3, 3, 4, 8, HALF), F32),
            pltpu.VMEM((8, 128), F32),
            pltpu.VMEM((8, 128), F32),
            pltpu.VMEM((16, D), BF16),
            pltpu.VMEM((8, 16, 256), BF16),
            *[pltpu.VMEM((2, 4, 4, 4, rows, 128), BF16) for rows in RS_ROWS],
            *[pltpu.VMEM((2, 2, 4, rows, 128), BF16) for rows in RS_ROWS],
            *[pltpu.VMEM((2, 2, 4, rows, 128), BF16) for rows in RS_ROWS],
            *[pltpu.VMEM((2, 4, 4, rows, 128), BF16) for rows in RS_ROWS],
            *[pltpu.VMEM((2, 4, 4, rows, 128), BF16) for rows in RS_ROWS],
            *[pltpu.VMEM((2, 3, 4, rows, 128), BF16) for rows in RS_ROWS],
            *[pltpu.VMEM((2, 3, rows, 128), BF16) for rows in RS_ROWS],
            dma, dma, dma, dma((75,)), dma((75,)), dma((16,)), dma((16,)), dma, dma,
            dma((54,)), dma((54,)), dma, dma, dma((72,)), dma((72,)), dma((8,)), dma((8,)), dma, dma,
        ],
        compiler_params=pltpu.CompilerParams(
            collective_id=0, has_side_effects=True, vmem_limit_bytes=48 * 1024 * 1024
        ),
    )(queries, passages, pool_rows, negatives)
    loss, gq, gp, gpool = pl.pallas_call(
        hand_on,
        out_shape=(jax.ShapeDtypeStruct((1, 1), F32), pieces, pieces, rows_out),
        in_specs=[vmem, vmem, vmem, vmem],
        out_specs=(smem, hbm, hbm, hbm),
        scratch_shapes=[dma((3,))],
        compiler_params=pltpu.CompilerParams(vmem_limit_bytes=8 * 1024 * 1024),
    )(loss, gq, gp, gpool)
    return loss[0, 0], gq, gp, gpool


def solution(mesh):
    placed = (P("dp", "mp"), P("dp", "mp"), P(("dp", "mp"), None), P(("dp", "mp"), None))
    return jax.shard_map(
        body,
        mesh=mesh,
        in_specs=placed,
        out_specs=(P(), P("dp", "mp"), P("dp", "mp"), P(("dp", "mp"), None)),
        check_vma=False,
    )
```

```python
import jax
import jax.numpy as jnp
from jax import lax
from jax.experimental import pallas as pl
from jax.experimental.pallas import tpu as pltpu
from jax.sharding import PartitionSpec as P

MESH = pl.DeviceIdType.MESH
F32 = jnp.float32
BF16 = jnp.bfloat16

D = 4096
NEGS = 31
BATCH = 1024
ROWS = 512
PLANE = 512
SCALE = 1.0 / 64.0
ORDERS = ("xyz", "yzx", "zxy")
HALF = 256
AG_ROWS = 48
RS_ROWS = (48, 48, 32)
UNITS = (((0, 48, 0, 0),), ((0, 48, 1, 0),), ((48, 16, 0, 0), (48, 16, 1, 16)))
LOW = -1e30


def kernel(
    q_hbm, p_hbm, pool_ref, neg_hbm,
    loss_ref, gq_ref, gp_ref, gpool_ref,
    q_ref, p_ref, neg_ref, in_sem, ag0, ag1, ag2, pool, queries, pas_rx, scores, names, et, pet, wd, wx, cols_of,
    stats, loss_own, loss_sib, gp_sum, gp_tx, gp_rx,
    d0, d1, d2, hl0, hl1, hl2, hr0, hr1, hr2, fl0, fl1, fl2, fr0, fr1, fr2, r10, r11, r12, r20, r21, r22,
    local_sem, pool_send, pool_recv, ag_send, ag_recv, pas_send, pas_recv, q_send, q_recv,
    st_send, st_recv, w_send, w_recv, rs_send, rs_recv, gp_send, gp_recv, loss_send, loss_recv,
):
    dp = lax.axis_index("dp")
    mp = lax.axis_index("mp")
    core = lax.rem(dp, 2)
    at = {"x": dp // 2, "y": lax.rem(mp, 4), "z": mp // 4}
    zy = mp
    sib = (at["x"] * 2 + 1 - core, mp)

    def peer(axis, delta):
        there = dict(at)
        there[axis] = lax.rem(at[axis] + delta, 4)
        return (there["x"] * 2 + core, there["z"] * 4 + there["y"])

    def send(src, dst, send_sem, recv_sem, device):
        copy = pltpu.make_async_remote_copy(
            src_ref=src, dst_ref=dst, send_sem=send_sem, recv_sem=recv_sem,
            device_id=device, device_id_type=MESH,
        )
        copy.start()
        return copy

    def arrived(ref, sem):
        pltpu.make_async_copy(ref, ref, sem).wait()

    barrier = pltpu.get_barrier_semaphore()
    for axis in "xyz":
        for delta in (1, 2, 3):
            pl.semaphore_signal(barrier, inc=1, device_id=peer(axis, delta), device_id_type=MESH)
    pl.semaphore_signal(barrier, inc=1, device_id=sib, device_id_type=MESH)

    pending = []
    inputs = [
        pltpu.make_async_copy(src, dst, in_sem.at[i])
        for i, (src, dst) in enumerate(((q_hbm, q_ref), (neg_hbm, neg_ref), (p_hbm, p_ref)))
    ]
    for copy in inputs:
        copy.start()
    own_pool = pltpu.make_async_copy(pool_ref, pool.at[0:ROWS], local_sem)
    own_pool.start()

    ags = (ag0, ag1, ag2)

    def slot(part):
        a, b, c = ORDERS[part]
        return at[c], at[b], at[a]

    for copy in inputs:
        copy.wait()
    ids = neg_ref[...]
    high = (ids >> 8).astype(F32)
    low = (ids & 255).astype(F32)
    tile = jnp.concatenate([high, low], axis=0)
    tile = jnp.concatenate([tile, jnp.zeros((16, 128 - NEGS), F32)], axis=1).astype(BF16)
    for s in range(2):
        for part in range(3):
            c, b, a = slot(part)
            for row, rows, h, o in UNITS[part]:
                piece = q_ref[64 * s + row : 64 * s + row + rows, 128 * h : 128 * h + 128]
                ags[part][s, c, b, a, o : o + rows] = piece
        c, b, a = slot(2)
        ag2[s, c, b, a, 32:48] = tile
    pl.semaphore_wait(barrier, 10)

    for part in range(3):
        c, b, a = slot(part)
        own = ags[part].at[:, c, b, a]
        for delta in (1, 2, 3):
            k = part * 25 + delta - 1
            pending.append(send(own, own, ag_send.at[k], ag_recv.at[k], peer(ORDERS[part][0], delta)))
    pool_copy = send(pool_ref, pool.at[ROWS : 2 * ROWS], pool_send, pool_recv, sib)

    def third(part, view, k):
        axis = ORDERS[part][2]
        pending.append(send(view, view, ag_send.at[k], ag_recv.at[k], peer(axis, 1)))
        pending.append(send(view, view, ag_send.at[k + 1], ag_recv.at[k + 1], peer(axis, 3)))

    def second(part, s):
        c, b, a = slot(part)
        line = ags[part].at[s, c, b]
        for delta in (1, 2, 3):
            k = part * 25 + 3 + 3 * s + delta - 1
            pending.append(send(line, line, ag_send.at[k], ag_recv.at[k], peer(ORDERS[part][1], delta)))

    def second_arrived(part, s):
        c, b, a = slot(part)
        for delta in (1, 2, 3):
            arrived(ags[part].at[s, c, lax.rem(b + 4 - delta, 4)], ag_recv.at[part * 25 + 3 + 3 * s + delta - 1])

    for part in range(3):
        c, b, a = slot(part)
        buf = ags[part]
        for delta in (1, 2, 3):
            arrived(buf.at[:, c, b, lax.rem(a + 4 - delta, 4)], ag_recv.at[part * 25 + delta - 1])
        second(part, 0)
        third(part, buf.at[0, c, b], part * 25 + 9)
    for part in range(3):
        second(part, 1)
    for part in range(3):
        c, b, a = slot(part)
        buf = ags[part]
        second_arrived(part, 0)
        for j in (1, 2, 3):
            third(part, buf.at[0, c, lax.rem(b + j, 4)], part * 25 + 9 + 2 * j)

    for t in range(8):
        for other in range(2):
            chip = core * 8 + t
            target = (at["x"] * 2 + other, chip)
            me = jnp.logical_and(chip == zy, core == other)
            src = p_ref.at[16 * t : 16 * t + 16]
            dst = pas_rx.at[zy]
            k = t * 2 + other

            @pl.when(me)
            def _():
                pltpu.make_async_copy(src, dst, pas_recv.at[zy]).start()

            @pl.when(jnp.logical_not(me))
            def _():
                send(src, dst, pas_send.at[k], pas_recv.at[zy], target)

    for part in range(3):
        c, b, a = slot(part)
        buf = ags[part]
        axis = ORDERS[part][2]
        before, after = lax.rem(c + 3, 4), lax.rem(c + 1, 4)
        for j in range(4):
            bb = lax.rem(b + j, 4)
            k = part * 25 + 9 + 2 * j
            kf = part * 25 + 17 + j
            arrived(buf.at[0, before, bb], ag_recv.at[k])
            arrived(buf.at[0, after, bb], ag_recv.at[k + 1])
            view = buf.at[0, before if j < 2 else after, bb]
            pending.append(send(view, view, ag_send.at[kf], ag_recv.at[kf], peer(axis, 1 if j < 2 else 3)))
    for part in range(3):
        c, b, a = slot(part)
        second_arrived(part, 1)
        third(part, ags[part].at[1, c], part * 25 + 21)

    def forward_last():
        for part in range(3):
            c, b, a = slot(part)
            buf = ags[part]
            axis = ORDERS[part][2]
            before, after = lax.rem(c + 3, 4), lax.rem(c + 1, 4)
            k = part * 25 + 21
            arrived(buf.at[1, before], ag_recv.at[k])
            view = buf.at[1, before, 0:2]
            pending.append(send(view, view, ag_send.at[k + 2], ag_recv.at[k + 2], peer(axis, 1)))
            arrived(buf.at[1, after], ag_recv.at[k + 1])
            view = buf.at[1, after, 2:4]
            pending.append(send(view, view, ag_send.at[k + 3], ag_recv.at[k + 3], peer(axis, 3)))

    contract = (((1,), (1,)), ((), ()))

    def assemble(s):
        def one(i, _):
            z, y = i // 4, lax.rem(i, 4)
            for x in range(4):
                where = {"x": x, "y": y, "z": z}
                for part in range(3):
                    aa, bb, cc = ORDERS[part]
                    for row, rows, h, o in UNITS[part]:
                        start = s * PLANE + x * 64 + row
                        cols = pl.ds(pl.multiple_of(i * 256 + 128 * h, 128), 128)
                        piece = ags[part][s, where[cc], where[bb], where[aa], o : o + rows]
                        queries[start : start + rows, cols] = piece
            return 0

        lax.fori_loop(0, 16, one, 0)

    mine = dp * 16 + mp
    theirs = (at["x"] * 2 + 1 - core) * 16 + mp
    sub = lax.broadcasted_iota(jnp.int32, (128, 128), 0)

    def find_names(s):
        for pair in range(2):
            pieces = []
            for x in (2 * pair, 2 * pair + 1):
                for i in range(8 * s, 8 * s + 8):
                    where = {"x": x, "y": i % 4, "z": i // 4}
                    aa, bb, cc = ORDERS[2]
                    tile = ag2[0, where[cc], where[bb], where[aa], 32:48].astype(F32)
                    pieces.append(tile[0:8] * 256.0 + tile[8:16])
            named = jnp.concatenate(pieces, axis=0).T[0:32].astype(jnp.int32)
            owner = named >> 9
            field = ((named >> 7) & 3) * 4
            bit = jnp.where(
                owner == mine, jnp.left_shift(1, field),
                jnp.where(owner == theirs, jnp.left_shift(1, field + 16), 0),
            )
            hi = named & 127
            packed = jnp.zeros((128, 128), jnp.int32)
            for k in range(NEGS):
                packed = packed + jnp.where(sub == hi[k : k + 1], bit[k : k + 1], 0)
            names[s, :, 128 * pair : 128 * pair + 128] = packed

    def score(s):
        rows = slice(s * PLANE, s * PLANE + HALF)

        def one(i, _):
            cols = pl.ds(pl.multiple_of(i * 2048, 2048), 2048)
            scores[s] += lax.dot_general(pool[:, cols], queries[rows, cols], contract, preferred_element_type=F32)
            return 0

        scores[s] = jnp.zeros((2 * ROWS + 16, HALF), F32)
        lax.fori_loop(0, 2, one, 0)

    lane = lax.broadcasted_iota(jnp.int32, (16, HALF), 1)
    psub = lax.broadcasted_iota(jnp.int32, (16, HALF), 0)
    in_plane = core == zy // 8
    row128 = lax.rem(zy, 8) * 16

    def same_of(s):
        held = jnp.logical_and(in_plane, row128 // 64 == s)
        first = jnp.where(held, at["x"] * 64 + lax.rem(row128, 64), -1024)
        return lane == first + psub

    def soften(s):
        def count_of(f):
            return (names[s] >> (4 * f)) & 15

        ps = scores[s, 2 * ROWS : 2 * ROWS + 16] * SCALE
        pos = jnp.sum(jnp.where(same_of(s), ps, 0.0), axis=0, keepdims=True)
        top = jnp.max(ps, axis=0, keepdims=True)
        for f in range(8):
            v = jnp.where(count_of(f) > 0, scores[s, 128 * f : 128 * f + 128] * SCALE, LOW)
            scores[s, 128 * f : 128 * f + 128] = v
            top = jnp.maximum(top, jnp.max(v, axis=0, keepdims=True))
        pe = jnp.exp(ps - top)
        scores[s, 2 * ROWS : 2 * ROWS + 16] = pe
        total = jnp.sum(pe, axis=0, keepdims=True)
        for f in range(8):
            e = jnp.exp(scores[s, 128 * f : 128 * f + 128] - top) * count_of(f).astype(F32)
            scores[s, 128 * f : 128 * f + 128] = e
            total = total + jnp.sum(e, axis=0, keepdims=True)
            et[s, :, 128 * f : 128 * f + 128] = e.T.astype(BF16)
        pet[s] = pe.T.astype(BF16)
        return top, total, pos

    filler = jnp.zeros((5, HALF), F32)

    def stats_send(s, n, tiles):
        for part in range(3):
            axis = ORDERS[part][2 - n]
            g = at[axis]
            stats[s, n, part, g] = jnp.concatenate(list(tiles[part]) + [filler], axis=0)
            ref = stats.at[s, n, part, g]
            for delta in (1, 2, 3):
                k = ((s * 3 + n) * 3 + part) * 3 + delta - 1
                pending.append(send(ref, ref, st_send.at[k], st_recv.at[k], peer(axis, delta)))

    def stats_meet(s, n):
        met = []
        for part in range(3):
            g = at[ORDERS[part][2 - n]]
            for delta in (1, 2, 3):
                k = ((s * 3 + n) * 3 + part) * 3 + delta - 1
                arrived(stats.at[s, n, part, lax.rem(g + 4 - delta, 4)], st_recv.at[k])
            tiles = [stats[s, n, part, j] for j in range(4)]
            best = tiles[0][0:1]
            for j in range(1, 4):
                best = jnp.maximum(best, tiles[j][0:1])
            summed = jnp.zeros_like(best)
            positive = jnp.zeros_like(best)
            for j in range(4):
                summed = summed + tiles[j][1:2] * jnp.exp(tiles[j][0:1] - best)
                positive = positive + tiles[j][2:3]
            met.append((best, summed, positive))
        return met

    third_part = lax.rem(lax.broadcasted_iota(jnp.int32, (1, HALF), 1), 64) >= 48

    def place_column(s, index, rows):
        for table, row in enumerate((jnp.where(third_part, rows[2], rows[0]), rows[1])):
            wide = jnp.broadcast_to(row, (128, HALF))
            for x in range(2):
                cols_of[s, index, table, 128 * x : 128 * x + 128] = wide[:, 128 * x : 128 * x + 128].T

    ds = (d0, d1, d2)

    def back(s):
        wide = 8

        def one(i, _):
            cols = pl.ds(pl.multiple_of(i * (256 * wide), 256 * wide), 256 * wide)
            acc = jnp.dot(et[s], pool[0 : 2 * ROWS, cols], preferred_element_type=F32)
            acc = (acc + jnp.dot(pet[s], pool[2 * ROWS : 2 * ROWS + 16, cols], preferred_element_type=F32)).astype(BF16)
            for j in range(wide):
                z, y = (i * wide + j) // 4, lax.rem(i * wide + j, 4)
                for x in range(4):
                    where = {"x": x, "y": y, "z": z}
                    for part in range(3):
                        aa, bb, cc = ORDERS[part]
                        for row, rows, h, o in UNITS[part]:
                            left = 256 * j + 128 * h
                            piece = acc[x * 64 + row : x * 64 + row + rows, left : left + 128]
                            ds[part][s, where[cc], where[bb], where[aa], o : o + rows] = piece
            return 0

        lax.fori_loop(0, 16 // wide, one, 0)

    hls, hrs, fls, frs = (hl0, hl1, hl2), (hr0, hr1, hr2), (fl0, fl1, fl2), (fr0, fr1, fr2)
    r1s, r2s = (r10, r11, r12), (r20, r21, r22)

    def scatter_key(part, s):
        return (part * 2 + s) * 12

    def scatter_start(s):
        for part in range(3):
            c, b, a = slot(part)
            axis = ORDERS[part][2]
            k = scatter_key(part, s)
            d = ds[part]
            far, before, after = lax.rem(c + 2, 4), lax.rem(c + 3, 4), lax.rem(c + 1, 4)
            right, left = peer(axis, 1), peer(axis, 3)
            pending.append(send(d.at[s, far, 0:2], hls[part].at[s], rs_send.at[k], rs_recv.at[k], right))
            pending.append(send(d.at[s, far, 2:4], hrs[part].at[s], rs_send.at[k + 1], rs_recv.at[k + 1], left))
            pending.append(send(d.at[s, after, 2:4], fls[part].at[s, 2:4], rs_send.at[k + 2], rs_recv.at[k + 2], right))
            pending.append(send(d.at[s, before, 0:2], frs[part].at[s, 0:2], rs_send.at[k + 3], rs_recv.at[k + 3], left))

    def factor_rows(part, s, index, c, b, a):
        x = dict(zip(ORDERS[part], (a, b, c)))["x"]
        if part < 2:
            return cols_of[s, index, part, pl.ds(pl.multiple_of(x * 64, 16), 48)]
        v = cols_of[s, index, 0, pl.ds(pl.multiple_of(x * 64 + 48, 16), 16)]
        return jnp.concatenate([v, v], axis=0)

    def scatter_forward(s):
        for part in range(3):
            c, b, a = slot(part)
            axis = ORDERS[part][2]
            k = scatter_key(part, s)
            d, hl, hr = ds[part], hls[part], hrs[part]
            before, after = lax.rem(c + 3, 4), lax.rem(c + 1, 4)

            def add(i, _, block, base, rx, column):
                bb, aa = i // 4, lax.rem(i, 4)
                own = d[s, block, base + bb, aa].astype(F32) * factor_rows(part, s, 0, block, base + bb, aa)
                other = rx[s, bb, aa].astype(F32) * factor_rows(part, s, column, block, base + bb, aa)
                d[s, block, base + bb, aa] = (own + other).astype(BF16)
                return 0

            arrived(hl.at[s], rs_recv.at[k])
            lax.fori_loop(0, 8, lambda i, t: add(i, t, after, 0, hl, 1), 0)
            pending.append(send(
                d.at[s, after, 0:2], fls[part].at[s, 0:2], rs_send.at[k + 4], rs_recv.at[k + 4], peer(axis, 1)
            ))
            arrived(hr.at[s], rs_recv.at[k + 1])
            lax.fori_loop(0, 8, lambda i, t: add(i, t, before, 2, hr, 2), 0)
            pending.append(send(
                d.at[s, before, 2:4], frs[part].at[s, 2:4], rs_send.at[k + 5], rs_recv.at[k + 5], peer(axis, 3)
            ))

    def scatter_second(s):
        for part in range(3):
            c, b, a = slot(part)
            k = scatter_key(part, s)
            d, fl, fr = ds[part], fls[part], frs[part]
            arrived(fl.at[s, 2:4], rs_recv.at[k + 2])
            arrived(fr.at[s, 0:2], rs_recv.at[k + 3])
            arrived(fl.at[s, 0:2], rs_recv.at[k + 4])
            arrived(fr.at[s, 2:4], rs_recv.at[k + 5])

            def low_half(i, _):
                bb, aa = i // 4, lax.rem(i, 4)
                total = d[s, c, bb, aa].astype(F32) * factor_rows(part, s, 0, c, bb, aa)
                total = total + fr[s, bb, aa].astype(F32) * factor_rows(part, s, 2, c, bb, aa) + fl[s, bb, aa].astype(F32)
                d[s, c, bb, aa] = (total * factor_rows(part, s, 3, c, bb, aa)).astype(BF16)
                return 0

            def high_half(i, _):
                bb, aa = i // 4 + 2, lax.rem(i, 4)
                total = d[s, c, bb, aa].astype(F32) * factor_rows(part, s, 0, c, bb, aa)
                total = total + fl[s, bb, aa].astype(F32) * factor_rows(part, s, 1, c, bb, aa) + fr[s, bb, aa].astype(F32)
                d[s, c, bb, aa] = (total * factor_rows(part, s, 3, c, bb, aa)).astype(BF16)
                return 0

            lax.fori_loop(0, 8, low_half, 0)
            lax.fori_loop(0, 8, high_half, 0)
            for delta in (1, 2, 3):
                pending.append(send(
                    d.at[s, c, lax.rem(b + delta, 4)], r1s[part].at[s, delta - 1],
                    rs_send.at[k + 5 + delta], rs_recv.at[k + 5 + delta], peer(ORDERS[part][1], delta),
                ))

    def scatter_third(s):
        for part in range(3):
            c, b, a = slot(part)
            k = scatter_key(part, s)
            d, r1 = ds[part], r1s[part]
            for delta in (1, 2, 3):
                arrived(r1.at[s, delta - 1], rs_recv.at[k + 5 + delta])
            for aa in range(4):
                total = d[s, c, b, aa].astype(F32)
                for j in range(3):
                    total = total + r1[s, j, aa].astype(F32)
                d[s, c, b, aa] = (total * factor_rows(part, s, 4, c, b, aa)).astype(BF16)
            for delta in (1, 2, 3):
                pending.append(send(
                    d.at[s, c, b, lax.rem(a + delta, 4)], r2s[part].at[s, delta - 1],
                    rs_send.at[k + 8 + delta], rs_recv.at[k + 8 + delta], peer(ORDERS[part][0], delta),
                ))

    def scatter_end(s):
        for part in range(3):
            c, b, a = slot(part)
            k = scatter_key(part, s)
            d, r2 = ds[part], r2s[part]
            total = d[s, c, b, a].astype(F32)
            for delta in (1, 2, 3):
                arrived(r2.at[s, delta - 1], rs_recv.at[k + 8 + delta])
                total = total + r2[s, delta - 1].astype(F32)
            total = total * factor_rows(part, s, 5, c, b, a)
            for row, rows, h, o in UNITS[part]:
                there = (slice(64 * s + row, 64 * s + row + rows), slice(128 * h, 128 * h + 128))
                gq_ref[there] = (total[o : o + rows] - p_ref[there].astype(F32) * (SCALE / BATCH)).astype(BF16)

    def first_factors(s, top, met):
        best = [met[part][0] for part in range(3)]
        place_column(s, 0, [jnp.exp(top - best[part]) for part in range(3)])
        for index, delta in ((1, 3), (2, 1)):
            rows = []
            for part in range(3):
                there = lax.rem(at[ORDERS[part][2]] + delta, 4)
                rows.append(jnp.exp(stats[s, 0, part, there][0:1] - best[part]))
            place_column(s, index, rows)

    def next_factors(s, index, met, wider):
        place_column(s, index, [jnp.exp(met[part][0] - wider[part][0]) for part in range(3)])

    def finish_stats(s, met, top):
        best, summed, positive = met[0]
        log_total = best + jnp.log(summed)
        place_column(s, 5, [jnp.exp(best - log_total) * (SCALE / BATCH)] * 3)
        return jnp.exp(top - log_total) / BATCH, jnp.sum(log_total - positive, axis=1, keepdims=True)

    def weigh(s, factor):
        own = slice(s * PLANE, s * PLANE + HALF)
        wp = scores[s, 2 * ROWS : 2 * ROWS + 16] * factor - jnp.where(same_of(s), 1.0 / BATCH, 0.0)
        wp = wp.astype(BF16)
        wx[s, 0:ROWS] = (scores[s, ROWS : 2 * ROWS] * factor).astype(BF16)
        wx[s, ROWS : ROWS + 16] = wp
        wd[0:ROWS, own] = (scores[s, 0:ROWS] * factor).astype(BF16)
        wd[ROWS : ROWS + 16, own] = wp

    def there(s, plane):
        return slice(s * PLANE + plane * HALF, s * PLANE + plane * HALF + HALF)

    def weights_send(s):
        return send(wx.at[s], wd.at[:, there(s, 1)], w_send.at[s], w_recv.at[s], sib)

    def pool_grad(s):
        arrived(queries.at[there(s, 1)], q_recv.at[s])
        arrived(wx.at[s], w_recv.at[s])
        both = slice(s * PLANE, s * PLANE + PLANE)

        def one(i, _):
            cols = pl.ds(pl.multiple_of(i * 1024, 1024), 1024)
            acc = jnp.dot(wd[:, both], queries[both, cols], preferred_element_type=F32) * SCALE
            if s == 0:
                gpool_ref[:, cols] = acc[0:ROWS].astype(BF16)
                gp_sum[:, cols] = acc[ROWS : ROWS + 16]
            else:
                gpool_ref[:, cols] = (gpool_ref[:, cols].astype(F32) + acc[0:ROWS]).astype(BF16)
                gp_tx[:, cols] = (gp_sum[:, cols] + acc[ROWS : ROWS + 16]).astype(BF16)
            return 0

        lax.fori_loop(0, 4, one, 0)

    for part in range(3):
        c, b, a = slot(part)
        far = lax.rem(c + 2, 4)
        for j in range(4):
            arrived(ags[part].at[0, far, lax.rem(b + j, 4)], ag_recv.at[part * 25 + 17 + j])
    assemble(0)
    find_names(0)
    own_pool.wait()
    arrived(pool.at[ROWS : 2 * ROWS], pool_recv)
    for i in range(16):
        arrived(pas_rx.at[i], pas_recv.at[i])
        pool[2 * ROWS : 2 * ROWS + 16, 256 * i : 256 * i + 256] = pas_rx[i]
    score(0)
    forward_last()
    top_a, total_a, pos_a = soften(0)
    stats_send(0, 0, [(top_a, total_a, pos_a)] * 3)
    back(0)
    scatter_start(0)

    find_names(1)
    for part in range(3):
        c, b, a = slot(part)
        far = lax.rem(c + 2, 4)
        arrived(ags[part].at[1, far, 0:2], ag_recv.at[part * 25 + 23])
        arrived(ags[part].at[1, far, 2:4], ag_recv.at[part * 25 + 24])
    assemble(1)
    q_copies = [
        send(queries.at[there(s, 0)], queries.at[there(s, 1)], q_send.at[s], q_recv.at[s], sib) for s in range(2)
    ]
    score(1)
    met_a1 = stats_meet(0, 0)
    stats_send(0, 1, met_a1)
    first_factors(0, top_a, met_a1)
    scatter_forward(0)
    top_b, total_b, pos_b = soften(1)
    stats_send(1, 0, [(top_b, total_b, pos_b)] * 3)
    back(1)
    scatter_start(1)

    met_a2 = stats_meet(0, 1)
    stats_send(0, 2, met_a2)
    next_factors(0, 3, met_a1, met_a2)
    scatter_second(0)
    met_b1 = stats_meet(1, 0)
    stats_send(1, 1, met_b1)
    first_factors(1, top_b, met_b1)
    scatter_forward(1)
    met_a3 = stats_meet(0, 2)
    next_factors(0, 4, met_a2, met_a3)
    factor_a, loss_a = finish_stats(0, met_a3, top_a)
    weigh(0, factor_a)
    w_copies = [weights_send(0)]
    scatter_third(0)
    met_b2 = stats_meet(1, 1)
    stats_send(1, 2, met_b2)
    next_factors(1, 3, met_b1, met_b2)
    pool_grad(0)
    scatter_second(1)
    met_b3 = stats_meet(1, 2)
    next_factors(1, 4, met_b2, met_b3)
    factor_b, loss_b = finish_stats(1, met_b3, top_b)
    weigh(1, factor_b)
    w_copies.append(weights_send(1))
    loss_own[...] = jnp.broadcast_to(loss_a + loss_b, (8, 128))
    loss_copy = send(loss_own, loss_sib, loss_send, loss_recv, sib)

    pool_grad(1)

    plane_of = zy // 8
    for t in range(8):
        there = core * 8 + t
        target = (at["x"] * 2 + plane_of, there)
        me = jnp.logical_and(there == zy, plane_of == core)
        src = gp_tx.at[:, pl.ds(pl.multiple_of(there * 256, 256), 256)]
        place = lax.rem(zy, 8)

        @pl.when(me)
        def _():
            pltpu.make_async_copy(src, gp_rx.at[place], gp_recv.at[place]).start()

        @pl.when(jnp.logical_not(me))
        def _():
            send(src, gp_rx.at[place], gp_send.at[t], gp_recv.at[place], target)

    scatter_third(1)
    scatter_end(0)
    scatter_end(1)

    for i in range(8):
        arrived(gp_rx.at[i], gp_recv.at[i])
        gp_ref[16 * i : 16 * i + 16] = gp_rx[i]
    arrived(loss_sib, loss_recv)
    loss_ref[...] = (loss_own[...] + loss_sib[...]) / BATCH

    for copy in pending:
        copy.wait_send()
    for copy in (pool_copy, loss_copy, *q_copies, *w_copies):
        copy.wait_send()
    for t in range(8):
        for other in range(2):
            chip = core * 8 + t
            me = jnp.logical_and(chip == zy, core == other)

            @pl.when(jnp.logical_not(me))
            def _():
                arrived(p_ref.at[16 * t : 16 * t + 16], pas_send.at[t * 2 + other])

        me = jnp.logical_and(core * 8 + t == zy, plane_of == core)

        @pl.when(jnp.logical_not(me))
        def _():
            arrived(gp_rx.at[0], gp_send.at[t])


def hand_on(loss_in, gq_in, gp_in, gpool_in, loss_out, gq_out, gp_out, gpool_out, sem):
    copies = [
        pltpu.make_async_copy(src, dst, sem.at[i])
        for i, (src, dst) in enumerate(((gpool_in, gpool_out), (gq_in, gq_out), (gp_in, gp_out)))
    ]
    for copy in copies:
        copy.start()
    loss_out[0, 0] = loss_in[0, 0]
    for copy in copies:
        copy.wait()


def body(queries, passages, pool_rows, negatives):
    vmem = pl.BlockSpec(memory_space=pltpu.VMEM)
    smem = pl.BlockSpec(memory_space=pltpu.SMEM)
    hbm = pl.BlockSpec(memory_space=pltpu.HBM)
    dma = pltpu.SemaphoreType.DMA
    pieces = jax.ShapeDtypeStruct((128, 256), BF16)
    rows_out = jax.ShapeDtypeStruct((ROWS, D), BF16)
    loss, gq, gp, gpool = pl.pallas_call(
        kernel,
        out_shape=(jax.ShapeDtypeStruct((8, 128), F32), pieces, pieces, rows_out),
        in_specs=[hbm, hbm, hbm, hbm],
        out_specs=(vmem, vmem, vmem, vmem),
        scratch_shapes=[
            pltpu.VMEM((128, 256), BF16),
            pltpu.VMEM((128, 256), BF16),
            pltpu.VMEM((8, NEGS), jnp.int32),
            dma((3,)),
            *[pltpu.VMEM((2, 4, 4, 4, AG_ROWS, 128), BF16)] * 3,
            pltpu.VMEM((2 * ROWS + 16, D), BF16),
            pltpu.VMEM((2 * PLANE, D), BF16),
            pltpu.VMEM((16, 16, 256), BF16),
            pltpu.VMEM((2, 2 * ROWS + 16, HALF), F32),
            pltpu.VMEM((2, 128, HALF), jnp.int32),
            pltpu.VMEM((2, HALF, 2 * ROWS), BF16),
            pltpu.VMEM((2, HALF, 16), BF16),
            pltpu.VMEM((ROWS + 16, 2 * PLANE), BF16),
            pltpu.VMEM((2, ROWS + 16, HALF), BF16),
            pltpu.VMEM((2, 6, 2, HALF, 128), F32),
            pltpu.VMEM((2, 3, 3, 4, 8, HALF), F32),
            pltpu.VMEM((8, 128), F32),
            pltpu.VMEM((8, 128), F32),
            pltpu.VMEM((16, D), F32),
            pltpu.VMEM((16, D), BF16),
            pltpu.VMEM((8, 16, 256), BF16),
            *[pltpu.VMEM((2, 4, 4, 4, rows, 128), BF16) for rows in RS_ROWS],
            *[pltpu.VMEM((2, 2, 4, rows, 128), BF16) for rows in RS_ROWS],
            *[pltpu.VMEM((2, 2, 4, rows, 128), BF16) for rows in RS_ROWS],
            *[pltpu.VMEM((2, 4, 4, rows, 128), BF16) for rows in RS_ROWS],
            *[pltpu.VMEM((2, 4, 4, rows, 128), BF16) for rows in RS_ROWS],
            *[pltpu.VMEM((2, 3, 4, rows, 128), BF16) for rows in RS_ROWS],
            *[pltpu.VMEM((2, 3, rows, 128), BF16) for rows in RS_ROWS],
            dma, dma, dma, dma((75,)), dma((75,)), dma((16,)), dma((16,)), dma((2,)), dma((2,)),
            dma((54,)), dma((54,)), dma((2,)), dma((2,)), dma((72,)), dma((72,)), dma((8,)), dma((8,)), dma, dma,
        ],
        compiler_params=pltpu.CompilerParams(
            collective_id=0, has_side_effects=True, vmem_limit_bytes=48 * 1024 * 1024
        ),
    )(queries, passages, pool_rows, negatives)
    loss, gq, gp, gpool = pl.pallas_call(
        hand_on,
        out_shape=(jax.ShapeDtypeStruct((1, 1), F32), pieces, pieces, rows_out),
        in_specs=[vmem, vmem, vmem, vmem],
        out_specs=(smem, hbm, hbm, hbm),
        scratch_shapes=[dma((3,))],
        compiler_params=pltpu.CompilerParams(vmem_limit_bytes=8 * 1024 * 1024),
    )(loss, gq, gp, gpool)
    return loss[0, 0], gq, gp, gpool


def solution(mesh):
    placed = (P("dp", "mp"), P("dp", "mp"), P(("dp", "mp"), None), P(("dp", "mp"), None))
    return jax.shard_map(
        body,
        mesh=mesh,
        in_specs=placed,
        out_specs=(P(), P("dp", "mp"), P("dp", "mp"), P(("dp", "mp"), None)),
        check_vma=False,
    )
```

```python
import jax
import jax.numpy as jnp
from jax import lax
from jax.experimental import pallas as pl
from jax.experimental.pallas import tpu as pltpu
from jax.sharding import PartitionSpec as P

MESH = pl.DeviceIdType.MESH
F32 = jnp.float32
BF16 = jnp.bfloat16

D = 4096
NEGS = 31
BATCH = 1024
ROWS = 512
PLANE = 512
SCALE = 1.0 / 64.0
ORDERS = ("xyz", "yzx", "zxy")
HALF = 256
AG_ROWS = 48
RS_ROWS = (48, 48, 32)
UNITS = (((0, 48, 0, 0),), ((0, 48, 1, 0),), ((48, 16, 0, 0), (48, 16, 1, 16)))
LOW = -1e30


def kernel(
    q_hbm, p_hbm, pool_ref, neg_hbm,
    loss_ref, gq_ref, gp_ref, gpool_ref,
    q_ref, p_ref, neg_ref, in_sem, ag0, ag1, ag2, pool, queries, pas_rx, scores, names, et, pet, wd, wx, cols_of,
    stats, loss_own, loss_sib, gp_sum, gp_tx, gp_rx,
    d0, d1, d2, hl0, hl1, hl2, hr0, hr1, hr2, fl0, fl1, fl2, fr0, fr1, fr2, r10, r11, r12, r20, r21, r22,
    local_sem, pool_send, pool_recv, ag_send, ag_recv, pas_send, pas_recv, q_send, q_recv,
    st_send, st_recv, w_send, w_recv, rs_send, rs_recv, gp_send, gp_recv, loss_send, loss_recv,
):
    dp = lax.axis_index("dp")
    mp = lax.axis_index("mp")
    core = lax.rem(dp, 2)
    at = {"x": dp // 2, "y": lax.rem(mp, 4), "z": mp // 4}
    zy = mp
    sib = (at["x"] * 2 + 1 - core, mp)

    def peer(axis, delta):
        there = dict(at)
        there[axis] = lax.rem(at[axis] + delta, 4)
        return (there["x"] * 2 + core, there["z"] * 4 + there["y"])

    def send(src, dst, send_sem, recv_sem, device):
        copy = pltpu.make_async_remote_copy(
            src_ref=src, dst_ref=dst, send_sem=send_sem, recv_sem=recv_sem,
            device_id=device, device_id_type=MESH,
        )
        copy.start()
        return copy

    def arrived(ref, sem):
        pltpu.make_async_copy(ref, ref, sem).wait()

    barrier = pltpu.get_barrier_semaphore()
    for axis in "xyz":
        for delta in (1, 2, 3):
            pl.semaphore_signal(barrier, inc=1, device_id=peer(axis, delta), device_id_type=MESH)
    pl.semaphore_signal(barrier, inc=1, device_id=sib, device_id_type=MESH)

    pending = []
    inputs = [
        pltpu.make_async_copy(src, dst, in_sem.at[i])
        for i, (src, dst) in enumerate(((q_hbm, q_ref), (neg_hbm, neg_ref), (p_hbm, p_ref)))
    ]
    for copy in inputs:
        copy.start()
    own_pool = pltpu.make_async_copy(pool_ref, pool.at[0:ROWS], local_sem)
    own_pool.start()

    ags = (ag0, ag1, ag2)

    def slot(part):
        a, b, c = ORDERS[part]
        return at[c], at[b], at[a]

    for copy in inputs:
        copy.wait()
    ids = neg_ref[...]
    high = (ids >> 8).astype(F32)
    low = (ids & 255).astype(F32)
    tile = jnp.concatenate([high, low], axis=0)
    tile = jnp.concatenate([tile, jnp.zeros((16, 128 - NEGS), F32)], axis=1).astype(BF16)
    for s in range(2):
        for part in range(3):
            c, b, a = slot(part)
            for row, rows, h, o in UNITS[part]:
                piece = q_ref[64 * s + row : 64 * s + row + rows, 128 * h : 128 * h + 128]
                ags[part][s, c, b, a, o : o + rows] = piece
        c, b, a = slot(2)
        ag2[s, c, b, a, 32:48] = tile
    pl.semaphore_wait(barrier, 10)

    for part in range(3):
        c, b, a = slot(part)
        own = ags[part].at[:, c, b, a]
        for delta in (1, 2, 3):
            k = part * 25 + delta - 1
            pending.append(send(own, own, ag_send.at[k], ag_recv.at[k], peer(ORDERS[part][0], delta)))
    pool_copy = send(pool_ref, pool.at[ROWS : 2 * ROWS], pool_send, pool_recv, sib)

    def third(part, view, k):
        axis = ORDERS[part][2]
        pending.append(send(view, view, ag_send.at[k], ag_recv.at[k], peer(axis, 1)))
        pending.append(send(view, view, ag_send.at[k + 1], ag_recv.at[k + 1], peer(axis, 3)))

    def second(part, s):
        c, b, a = slot(part)
        line = ags[part].at[s, c, b]
        for delta in (1, 2, 3):
            k = part * 25 + 3 + 3 * s + delta - 1
            pending.append(send(line, line, ag_send.at[k], ag_recv.at[k], peer(ORDERS[part][1], delta)))

    def second_arrived(part, s):
        c, b, a = slot(part)
        for delta in (1, 2, 3):
            arrived(ags[part].at[s, c, lax.rem(b + 4 - delta, 4)], ag_recv.at[part * 25 + 3 + 3 * s + delta - 1])

    for part in range(3):
        c, b, a = slot(part)
        buf = ags[part]
        for delta in (1, 2, 3):
            arrived(buf.at[:, c, b, lax.rem(a + 4 - delta, 4)], ag_recv.at[part * 25 + delta - 1])
        second(part, 0)
        third(part, buf.at[0, c, b], part * 25 + 9)
    for part in range(3):
        second(part, 1)
    for part in range(3):
        c, b, a = slot(part)
        buf = ags[part]
        second_arrived(part, 0)
        for j in (1, 2, 3):
            third(part, buf.at[0, c, lax.rem(b + j, 4)], part * 25 + 9 + 2 * j)

    for t in range(8):
        for other in range(2):
            chip = core * 8 + t
            target = (at["x"] * 2 + other, chip)
            me = jnp.logical_and(chip == zy, core == other)
            src = p_ref.at[16 * t : 16 * t + 16]
            dst = pas_rx.at[zy]
            k = t * 2 + other

            @pl.when(me)
            def _():
                pltpu.make_async_copy(src, dst, pas_recv.at[zy]).start()

            @pl.when(jnp.logical_not(me))
            def _():
                send(src, dst, pas_send.at[k], pas_recv.at[zy], target)

    for part in range(3):
        c, b, a = slot(part)
        buf = ags[part]
        axis = ORDERS[part][2]
        before, after = lax.rem(c + 3, 4), lax.rem(c + 1, 4)
        for j in range(4):
            bb = lax.rem(b + j, 4)
            k = part * 25 + 9 + 2 * j
            kf = part * 25 + 17 + j
            arrived(buf.at[0, before, bb], ag_recv.at[k])
            arrived(buf.at[0, after, bb], ag_recv.at[k + 1])
            view = buf.at[0, before if j < 2 else after, bb]
            pending.append(send(view, view, ag_send.at[kf], ag_recv.at[kf], peer(axis, 1 if j < 2 else 3)))
    for part in range(3):
        c, b, a = slot(part)
        second_arrived(part, 1)
        third(part, ags[part].at[1, c], part * 25 + 21)

    def forward_last():
        for part in range(3):
            c, b, a = slot(part)
            buf = ags[part]
            axis = ORDERS[part][2]
            before, after = lax.rem(c + 3, 4), lax.rem(c + 1, 4)
            k = part * 25 + 21
            arrived(buf.at[1, before], ag_recv.at[k])
            view = buf.at[1, before, 0:2]
            pending.append(send(view, view, ag_send.at[k + 2], ag_recv.at[k + 2], peer(axis, 1)))
            arrived(buf.at[1, after], ag_recv.at[k + 1])
            view = buf.at[1, after, 2:4]
            pending.append(send(view, view, ag_send.at[k + 3], ag_recv.at[k + 3], peer(axis, 3)))

    contract = (((1,), (1,)), ((), ()))

    def assemble(s):
        def one(i, _):
            z, y = i // 4, lax.rem(i, 4)
            for x in range(4):
                where = {"x": x, "y": y, "z": z}
                for part in range(3):
                    aa, bb, cc = ORDERS[part]
                    for row, rows, h, o in UNITS[part]:
                        start = s * PLANE + x * 64 + row
                        cols = pl.ds(pl.multiple_of(i * 256 + 128 * h, 128), 128)
                        piece = ags[part][s, where[cc], where[bb], where[aa], o : o + rows]
                        queries[start : start + rows, cols] = piece
            return 0

        lax.fori_loop(0, 16, one, 0)

    mine = dp * 16 + mp
    theirs = (at["x"] * 2 + 1 - core) * 16 + mp
    sub = lax.broadcasted_iota(jnp.int32, (128, 128), 0)

    def find_names(s):
        for pair in range(2):
            pieces = []
            for x in (2 * pair, 2 * pair + 1):
                for i in range(8 * s, 8 * s + 8):
                    where = {"x": x, "y": i % 4, "z": i // 4}
                    aa, bb, cc = ORDERS[2]
                    tile = ag2[0, where[cc], where[bb], where[aa], 32:48].astype(F32)
                    pieces.append(tile[0:8] * 256.0 + tile[8:16])
            named = jnp.concatenate(pieces, axis=0).T[0:32].astype(jnp.int32)
            owner = named >> 9
            field = ((named >> 7) & 3) * 4
            bit = jnp.where(
                owner == mine, jnp.left_shift(1, field),
                jnp.where(owner == theirs, jnp.left_shift(1, field + 16), 0),
            )
            hi = named & 127
            packed = jnp.zeros((128, 128), jnp.int32)
            for k in range(NEGS):
                packed = packed + jnp.where(sub == hi[k : k + 1], bit[k : k + 1], 0)
            names[s, :, 128 * pair : 128 * pair + 128] = packed

    def score(s):
        rows = slice(s * PLANE, s * PLANE + HALF)

        def one(i, _):
            cols = pl.ds(pl.multiple_of(i * 4096, 4096), 4096)
            scores[s] += lax.dot_general(pool[:, cols], queries[rows, cols], contract, preferred_element_type=F32)
            return 0

        scores[s] = jnp.zeros((2 * ROWS + 16, HALF), F32)
        lax.fori_loop(0, 1, one, 0)

    lane = lax.broadcasted_iota(jnp.int32, (16, HALF), 1)
    psub = lax.broadcasted_iota(jnp.int32, (16, HALF), 0)
    in_plane = core == zy // 8
    row128 = lax.rem(zy, 8) * 16

    def same_of(s):
        held = jnp.logical_and(in_plane, row128 // 64 == s)
        first = jnp.where(held, at["x"] * 64 + lax.rem(row128, 64), -1024)
        return lane == first + psub

    def soften(s):
        def count_of(f):
            return (names[s] >> (4 * f)) & 15

        ps = scores[s, 2 * ROWS : 2 * ROWS + 16] * SCALE
        pos = jnp.sum(jnp.where(same_of(s), ps, 0.0), axis=0, keepdims=True)
        top = jnp.max(ps, axis=0, keepdims=True)
        for f in range(8):
            v = jnp.where(count_of(f) > 0, scores[s, 128 * f : 128 * f + 128] * SCALE, LOW)
            scores[s, 128 * f : 128 * f + 128] = v
            top = jnp.maximum(top, jnp.max(v, axis=0, keepdims=True))
        pe = jnp.exp(ps - top)
        scores[s, 2 * ROWS : 2 * ROWS + 16] = pe
        total = jnp.sum(pe, axis=0, keepdims=True)
        for f in range(8):
            e = jnp.exp(scores[s, 128 * f : 128 * f + 128] - top) * count_of(f).astype(F32)
            scores[s, 128 * f : 128 * f + 128] = e
            total = total + jnp.sum(e, axis=0, keepdims=True)
            et[s, :, 128 * f : 128 * f + 128] = e.T.astype(BF16)
        pet[s] = pe.T.astype(BF16)
        return top, total, pos

    filler = jnp.zeros((5, HALF), F32)

    def stats_send(s, n, tiles):
        for part in range(3):
            axis = ORDERS[part][2 - n]
            g = at[axis]
            stats[s, n, part, g] = jnp.concatenate(list(tiles[part]) + [filler], axis=0)
            ref = stats.at[s, n, part, g]
            for delta in (1, 2, 3):
                k = ((s * 3 + n) * 3 + part) * 3 + delta - 1
                pending.append(send(ref, ref, st_send.at[k], st_recv.at[k], peer(axis, delta)))

    def stats_meet(s, n):
        met = []
        for part in range(3):
            g = at[ORDERS[part][2 - n]]
            for delta in (1, 2, 3):
                k = ((s * 3 + n) * 3 + part) * 3 + delta - 1
                arrived(stats.at[s, n, part, lax.rem(g + 4 - delta, 4)], st_recv.at[k])
            tiles = [stats[s, n, part, j] for j in range(4)]
            best = tiles[0][0:1]
            for j in range(1, 4):
                best = jnp.maximum(best, tiles[j][0:1])
            summed = jnp.zeros_like(best)
            positive = jnp.zeros_like(best)
            for j in range(4):
                summed = summed + tiles[j][1:2] * jnp.exp(tiles[j][0:1] - best)
                positive = positive + tiles[j][2:3]
            met.append((best, summed, positive))
        return met

    third_part = lax.rem(lax.broadcasted_iota(jnp.int32, (1, HALF), 1), 64) >= 48

    def place_column(s, index, rows):
        for table, row in enumerate((jnp.where(third_part, rows[2], rows[0]), rows[1])):
            wide = jnp.broadcast_to(row, (128, HALF))
            for x in range(2):
                cols_of[s, index, table, 128 * x : 128 * x + 128] = wide[:, 128 * x : 128 * x + 128].T

    ds = (d0, d1, d2)

    def back(s):
        wide = 8

        def one(i, _):
            cols = pl.ds(pl.multiple_of(i * (256 * wide), 256 * wide), 256 * wide)
            acc = jnp.dot(et[s], pool[0 : 2 * ROWS, cols], preferred_element_type=F32)
            acc = (acc + jnp.dot(pet[s], pool[2 * ROWS : 2 * ROWS + 16, cols], preferred_element_type=F32)).astype(BF16)
            for j in range(wide):
                z, y = (i * wide + j) // 4, lax.rem(i * wide + j, 4)
                for x in range(4):
                    where = {"x": x, "y": y, "z": z}
                    for part in range(3):
                        aa, bb, cc = ORDERS[part]
                        for row, rows, h, o in UNITS[part]:
                            left = 256 * j + 128 * h
                            piece = acc[x * 64 + row : x * 64 + row + rows, left : left + 128]
                            ds[part][s, where[cc], where[bb], where[aa], o : o + rows] = piece
            return 0

        lax.fori_loop(0, 16 // wide, one, 0)

    hls, hrs, fls, frs = (hl0, hl1, hl2), (hr0, hr1, hr2), (fl0, fl1, fl2), (fr0, fr1, fr2)
    r1s, r2s = (r10, r11, r12), (r20, r21, r22)

    def scatter_key(part, s):
        return (part * 2 + s) * 12

    def scatter_start(s):
        for part in range(3):
            c, b, a = slot(part)
            axis = ORDERS[part][2]
            k = scatter_key(part, s)
            d = ds[part]
            far, before, after = lax.rem(c + 2, 4), lax.rem(c + 3, 4), lax.rem(c + 1, 4)
            right, left = peer(axis, 1), peer(axis, 3)
            pending.append(send(d.at[s, far, 0:2], hls[part].at[s], rs_send.at[k], rs_recv.at[k], right))
            pending.append(send(d.at[s, far, 2:4], hrs[part].at[s], rs_send.at[k + 1], rs_recv.at[k + 1], left))
        for part in range(3):
            c, b, a = slot(part)
            axis = ORDERS[part][2]
            k = scatter_key(part, s)
            d = ds[part]
            before, after = lax.rem(c + 3, 4), lax.rem(c + 1, 4)
            right, left = peer(axis, 1), peer(axis, 3)
            pending.append(send(d.at[s, after, 2:4], fls[part].at[s, 2:4], rs_send.at[k + 2], rs_recv.at[k + 2], right))
            pending.append(send(d.at[s, before, 0:2], frs[part].at[s, 0:2], rs_send.at[k + 3], rs_recv.at[k + 3], left))

    def factor_rows(part, s, index, c, b, a):
        x = dict(zip(ORDERS[part], (a, b, c)))["x"]
        if part < 2:
            return cols_of[s, index, part, pl.ds(pl.multiple_of(x * 64, 16), 48)]
        v = cols_of[s, index, 0, pl.ds(pl.multiple_of(x * 64 + 48, 16), 16)]
        return jnp.concatenate([v, v], axis=0)

    def scatter_forward(s):
        for part in range(3):
            c, b, a = slot(part)
            axis = ORDERS[part][2]
            k = scatter_key(part, s)
            d, hl, hr = ds[part], hls[part], hrs[part]
            before, after = lax.rem(c + 3, 4), lax.rem(c + 1, 4)

            def add(i, _, block, base, rx, column):
                bb, aa = i // 4, lax.rem(i, 4)
                own = d[s, block, base + bb, aa].astype(F32) * factor_rows(part, s, 0, block, base + bb, aa)
                other = rx[s, bb, aa].astype(F32) * factor_rows(part, s, column, block, base + bb, aa)
                d[s, block, base + bb, aa] = (own + other).astype(BF16)
                return 0

            arrived(hl.at[s], rs_recv.at[k])
            lax.fori_loop(0, 8, lambda i, t: add(i, t, after, 0, hl, 1), 0)
            pending.append(send(
                d.at[s, after, 0:2], fls[part].at[s, 0:2], rs_send.at[k + 4], rs_recv.at[k + 4], peer(axis, 1)
            ))
            arrived(hr.at[s], rs_recv.at[k + 1])
            lax.fori_loop(0, 8, lambda i, t: add(i, t, before, 2, hr, 2), 0)
            pending.append(send(
                d.at[s, before, 2:4], frs[part].at[s, 2:4], rs_send.at[k + 5], rs_recv.at[k + 5], peer(axis, 3)
            ))

    def scatter_second(s):
        for part in range(3):
            c, b, a = slot(part)
            k = scatter_key(part, s)
            d, fl, fr = ds[part], fls[part], frs[part]
            arrived(fl.at[s, 2:4], rs_recv.at[k + 2])
            arrived(fr.at[s, 0:2], rs_recv.at[k + 3])
            arrived(fl.at[s, 0:2], rs_recv.at[k + 4])
            arrived(fr.at[s, 2:4], rs_recv.at[k + 5])

            def low_half(i, _):
                bb, aa = i // 4, lax.rem(i, 4)
                total = d[s, c, bb, aa].astype(F32) * factor_rows(part, s, 0, c, bb, aa)
                total = total + fr[s, bb, aa].astype(F32) * factor_rows(part, s, 2, c, bb, aa) + fl[s, bb, aa].astype(F32)
                d[s, c, bb, aa] = (total * factor_rows(part, s, 3, c, bb, aa)).astype(BF16)
                return 0

            def high_half(i, _):
                bb, aa = i // 4 + 2, lax.rem(i, 4)
                total = d[s, c, bb, aa].astype(F32) * factor_rows(part, s, 0, c, bb, aa)
                total = total + fl[s, bb, aa].astype(F32) * factor_rows(part, s, 1, c, bb, aa) + fr[s, bb, aa].astype(F32)
                d[s, c, bb, aa] = (total * factor_rows(part, s, 3, c, bb, aa)).astype(BF16)
                return 0

            lax.fori_loop(0, 8, low_half, 0)
            lax.fori_loop(0, 8, high_half, 0)
            for delta in (1, 2, 3):
                pending.append(send(
                    d.at[s, c, lax.rem(b + delta, 4)], r1s[part].at[s, delta - 1],
                    rs_send.at[k + 5 + delta], rs_recv.at[k + 5 + delta], peer(ORDERS[part][1], delta),
                ))

    def scatter_third(s):
        for part in range(3):
            c, b, a = slot(part)
            k = scatter_key(part, s)
            d, r1 = ds[part], r1s[part]
            for delta in (1, 2, 3):
                arrived(r1.at[s, delta - 1], rs_recv.at[k + 5 + delta])
            for aa in range(4):
                total = d[s, c, b, aa].astype(F32)
                for j in range(3):
                    total = total + r1[s, j, aa].astype(F32)
                d[s, c, b, aa] = (total * factor_rows(part, s, 4, c, b, aa)).astype(BF16)
            for delta in (1, 2, 3):
                pending.append(send(
                    d.at[s, c, b, lax.rem(a + delta, 4)], r2s[part].at[s, delta - 1],
                    rs_send.at[k + 8 + delta], rs_recv.at[k + 8 + delta], peer(ORDERS[part][0], delta),
                ))

    def scatter_end(s):
        for part in range(3):
            c, b, a = slot(part)
            k = scatter_key(part, s)
            d, r2 = ds[part], r2s[part]
            total = d[s, c, b, a].astype(F32)
            for delta in (1, 2, 3):
                arrived(r2.at[s, delta - 1], rs_recv.at[k + 8 + delta])
                total = total + r2[s, delta - 1].astype(F32)
            total = total * factor_rows(part, s, 5, c, b, a)
            for row, rows, h, o in UNITS[part]:
                there = (slice(64 * s + row, 64 * s + row + rows), slice(128 * h, 128 * h + 128))
                gq_ref[there] = (total[o : o + rows] - p_ref[there].astype(F32) * (SCALE / BATCH)).astype(BF16)

    def first_factors(s, top, met):
        best = [met[part][0] for part in range(3)]
        place_column(s, 0, [jnp.exp(top - best[part]) for part in range(3)])
        for index, delta in ((1, 3), (2, 1)):
            rows = []
            for part in range(3):
                there = lax.rem(at[ORDERS[part][2]] + delta, 4)
                rows.append(jnp.exp(stats[s, 0, part, there][0:1] - best[part]))
            place_column(s, index, rows)

    def next_factors(s, index, met, wider):
        place_column(s, index, [jnp.exp(met[part][0] - wider[part][0]) for part in range(3)])

    def finish_stats(s, met, top):
        best, summed, positive = met[0]
        log_total = best + jnp.log(summed)
        place_column(s, 5, [jnp.exp(best - log_total) * (SCALE / BATCH)] * 3)
        return jnp.exp(top - log_total) / BATCH, jnp.sum(log_total - positive, axis=1, keepdims=True)

    def weigh(s, factor):
        own = slice(s * PLANE, s * PLANE + HALF)
        wp = scores[s, 2 * ROWS : 2 * ROWS + 16] * factor - jnp.where(same_of(s), 1.0 / BATCH, 0.0)
        wp = wp.astype(BF16)
        wx[s, 0:ROWS] = (scores[s, ROWS : 2 * ROWS] * factor).astype(BF16)
        wx[s, ROWS : ROWS + 16] = wp
        wd[0:ROWS, own] = (scores[s, 0:ROWS] * factor).astype(BF16)
        wd[ROWS : ROWS + 16, own] = wp

    def there(s, plane):
        return slice(s * PLANE + plane * HALF, s * PLANE + plane * HALF + HALF)

    def weights_send(s):
        return send(wx.at[s], wd.at[:, there(s, 1)], w_send.at[s], w_recv.at[s], sib)

    def pool_grad(s):
        arrived(queries.at[there(s, 1)], q_recv.at[s])
        arrived(wx.at[s], w_recv.at[s])
        both = slice(s * PLANE, s * PLANE + PLANE)

        def one(i, _):
            cols = pl.ds(pl.multiple_of(i * 1024, 1024), 1024)
            acc = jnp.dot(wd[:, both], queries[both, cols], preferred_element_type=F32) * SCALE
            if s == 0:
                gpool_ref[:, cols] = acc[0:ROWS].astype(BF16)
                gp_sum[:, cols] = acc[ROWS : ROWS + 16]
            else:
                gpool_ref[:, cols] = (gpool_ref[:, cols].astype(F32) + acc[0:ROWS]).astype(BF16)
                gp_tx[:, cols] = (gp_sum[:, cols] + acc[ROWS : ROWS + 16]).astype(BF16)
            return 0

        lax.fori_loop(0, 4, one, 0)

    for part in range(3):
        c, b, a = slot(part)
        far = lax.rem(c + 2, 4)
        for j in range(4):
            arrived(ags[part].at[0, far, lax.rem(b + j, 4)], ag_recv.at[part * 25 + 17 + j])
    assemble(0)
    find_names(0)
    own_pool.wait()
    arrived(pool.at[ROWS : 2 * ROWS], pool_recv)
    for i in range(16):
        arrived(pas_rx.at[i], pas_recv.at[i])
        pool[2 * ROWS : 2 * ROWS + 16, 256 * i : 256 * i + 256] = pas_rx[i]
    score(0)
    forward_last()
    top_a, total_a, pos_a = soften(0)
    stats_send(0, 0, [(top_a, total_a, pos_a)] * 3)
    back(0)
    scatter_start(0)

    find_names(1)
    for part in range(3):
        c, b, a = slot(part)
        far = lax.rem(c + 2, 4)
        arrived(ags[part].at[1, far, 0:2], ag_recv.at[part * 25 + 23])
        arrived(ags[part].at[1, far, 2:4], ag_recv.at[part * 25 + 24])
    assemble(1)
    q_copies = [
        send(queries.at[there(s, 0)], queries.at[there(s, 1)], q_send.at[s], q_recv.at[s], sib) for s in range(2)
    ]
    score(1)
    met_a1 = stats_meet(0, 0)
    stats_send(0, 1, met_a1)
    first_factors(0, top_a, met_a1)
    scatter_forward(0)
    top_b, total_b, pos_b = soften(1)
    stats_send(1, 0, [(top_b, total_b, pos_b)] * 3)
    back(1)
    scatter_start(1)

    met_a2 = stats_meet(0, 1)
    stats_send(0, 2, met_a2)
    next_factors(0, 3, met_a1, met_a2)
    scatter_second(0)
    met_b1 = stats_meet(1, 0)
    stats_send(1, 1, met_b1)
    first_factors(1, top_b, met_b1)
    scatter_forward(1)
    met_a3 = stats_meet(0, 2)
    next_factors(0, 4, met_a2, met_a3)
    factor_a, loss_a = finish_stats(0, met_a3, top_a)
    weigh(0, factor_a)
    w_copies = [weights_send(0)]
    scatter_third(0)
    met_b2 = stats_meet(1, 1)
    stats_send(1, 2, met_b2)
    next_factors(1, 3, met_b1, met_b2)
    pool_grad(0)
    scatter_second(1)
    met_b3 = stats_meet(1, 2)
    next_factors(1, 4, met_b2, met_b3)
    factor_b, loss_b = finish_stats(1, met_b3, top_b)
    weigh(1, factor_b)
    w_copies.append(weights_send(1))
    loss_own[...] = jnp.broadcast_to(loss_a + loss_b, (8, 128))
    loss_copy = send(loss_own, loss_sib, loss_send, loss_recv, sib)

    pool_grad(1)

    plane_of = zy // 8
    for t in range(8):
        there = core * 8 + t
        target = (at["x"] * 2 + plane_of, there)
        me = jnp.logical_and(there == zy, plane_of == core)
        src = gp_tx.at[:, pl.ds(pl.multiple_of(there * 256, 256), 256)]
        place = lax.rem(zy, 8)

        @pl.when(me)
        def _():
            pltpu.make_async_copy(src, gp_rx.at[place], gp_recv.at[place]).start()

        @pl.when(jnp.logical_not(me))
        def _():
            send(src, gp_rx.at[place], gp_send.at[t], gp_recv.at[place], target)

    scatter_third(1)
    scatter_end(0)
    scatter_end(1)

    for i in range(8):
        arrived(gp_rx.at[i], gp_recv.at[i])
        gp_ref[16 * i : 16 * i + 16] = gp_rx[i]
    arrived(loss_sib, loss_recv)
    loss_ref[...] = (loss_own[...] + loss_sib[...]) / BATCH

    for copy in pending:
        copy.wait_send()
    for copy in (pool_copy, loss_copy, *q_copies, *w_copies):
        copy.wait_send()
    for t in range(8):
        for other in range(2):
            chip = core * 8 + t
            me = jnp.logical_and(chip == zy, core == other)

            @pl.when(jnp.logical_not(me))
            def _():
                arrived(p_ref.at[16 * t : 16 * t + 16], pas_send.at[t * 2 + other])

        me = jnp.logical_and(core * 8 + t == zy, plane_of == core)

        @pl.when(jnp.logical_not(me))
        def _():
            arrived(gp_rx.at[0], gp_send.at[t])


def hand_on(loss_in, gq_in, gp_in, gpool_in, loss_out, gq_out, gp_out, gpool_out, sem):
    copies = [
        pltpu.make_async_copy(src, dst, sem.at[i])
        for i, (src, dst) in enumerate(((gpool_in, gpool_out), (gq_in, gq_out), (gp_in, gp_out)))
    ]
    for copy in copies:
        copy.start()
    loss_out[0, 0] = loss_in[0, 0]
    for copy in copies:
        copy.wait()


def body(queries, passages, pool_rows, negatives):
    vmem = pl.BlockSpec(memory_space=pltpu.VMEM)
    smem = pl.BlockSpec(memory_space=pltpu.SMEM)
    hbm = pl.BlockSpec(memory_space=pltpu.HBM)
    dma = pltpu.SemaphoreType.DMA
    pieces = jax.ShapeDtypeStruct((128, 256), BF16)
    rows_out = jax.ShapeDtypeStruct((ROWS, D), BF16)
    loss, gq, gp, gpool = pl.pallas_call(
        kernel,
        out_shape=(jax.ShapeDtypeStruct((8, 128), F32), pieces, pieces, rows_out),
        in_specs=[hbm, hbm, hbm, hbm],
        out_specs=(vmem, vmem, vmem, vmem),
        scratch_shapes=[
            pltpu.VMEM((128, 256), BF16),
            pltpu.VMEM((128, 256), BF16),
            pltpu.VMEM((8, NEGS), jnp.int32),
            dma((3,)),
            *[pltpu.VMEM((2, 4, 4, 4, AG_ROWS, 128), BF16)] * 3,
            pltpu.VMEM((2 * ROWS + 16, D), BF16),
            pltpu.VMEM((2 * PLANE, D), BF16),
            pltpu.VMEM((16, 16, 256), BF16),
            pltpu.VMEM((2, 2 * ROWS + 16, HALF), F32),
            pltpu.VMEM((2, 128, HALF), jnp.int32),
            pltpu.VMEM((2, HALF, 2 * ROWS), BF16),
            pltpu.VMEM((2, HALF, 16), BF16),
            pltpu.VMEM((ROWS + 16, 2 * PLANE), BF16),
            pltpu.VMEM((2, ROWS + 16, HALF), BF16),
            pltpu.VMEM((2, 6, 2, HALF, 128), F32),
            pltpu.VMEM((2, 3, 3, 4, 8, HALF), F32),
            pltpu.VMEM((8, 128), F32),
            pltpu.VMEM((8, 128), F32),
            pltpu.VMEM((16, D), F32),
            pltpu.VMEM((16, D), BF16),
            pltpu.VMEM((8, 16, 256), BF16),
            *[pltpu.VMEM((2, 4, 4, 4, rows, 128), BF16) for rows in RS_ROWS],
            *[pltpu.VMEM((2, 2, 4, rows, 128), BF16) for rows in RS_ROWS],
            *[pltpu.VMEM((2, 2, 4, rows, 128), BF16) for rows in RS_ROWS],
            *[pltpu.VMEM((2, 4, 4, rows, 128), BF16) for rows in RS_ROWS],
            *[pltpu.VMEM((2, 4, 4, rows, 128), BF16) for rows in RS_ROWS],
            *[pltpu.VMEM((2, 3, 4, rows, 128), BF16) for rows in RS_ROWS],
            *[pltpu.VMEM((2, 3, rows, 128), BF16) for rows in RS_ROWS],
            dma, dma, dma, dma((75,)), dma((75,)), dma((16,)), dma((16,)), dma((2,)), dma((2,)),
            dma((54,)), dma((54,)), dma((2,)), dma((2,)), dma((72,)), dma((72,)), dma((8,)), dma((8,)), dma, dma,
        ],
        compiler_params=pltpu.CompilerParams(
            collective_id=0, has_side_effects=True, vmem_limit_bytes=48 * 1024 * 1024
        ),
    )(*[pltpu.with_memory_space_constraint(v, pltpu.HBM) for v in (queries, passages, pool_rows, negatives)])
    loss, gq, gp, gpool = pl.pallas_call(
        hand_on,
        out_shape=(jax.ShapeDtypeStruct((1, 1), F32), pieces, pieces, rows_out),
        in_specs=[vmem, vmem, vmem, vmem],
        out_specs=(smem, hbm, hbm, hbm),
        scratch_shapes=[dma((3,))],
        compiler_params=pltpu.CompilerParams(vmem_limit_bytes=8 * 1024 * 1024),
    )(loss, gq, gp, gpool)
    return loss[0, 0], gq, gp, gpool


def solution(mesh):
    placed = (P("dp", "mp"), P("dp", "mp"), P(("dp", "mp"), None), P(("dp", "mp"), None))
    return jax.shard_map(
        body,
        mesh=mesh,
        in_specs=placed,
        out_specs=(P(), P("dp", "mp"), P("dp", "mp"), P(("dp", "mp"), None)),
        check_vma=False,
    )
```
